128 devices in a mesh: gx: 16 (over z_lo, y, core), gy: 8 (over x, z_hi).
Axes of the slice: x: 4, y: 4, z: 4 (z_hi: 2, z_lo: 2; z = z_hi * 2 + z_lo), core: 2. Of those that a mesh axis runs over, the one named last changes fastest.
Arguments:
- probability: float32 [16, 16, 64, 2048], P('gx', None, None, 'gy'), may hold values from 0 to 1
- extent: int32 [4], replicated, may hold values from 4 to 1019, as said below
- slab_width: int32 [4], replicated, may hold values from 1 to 4, as said below
- rate_const: float32 [8], replicated, may hold values from 0.25 to 1.5
- hill_const: float32 [8], replicated, may hold values from 0.1 to 1
- stoichiometry: int32 [8, 4], replicated, may hold values from -1 to 1, as said below
- new_owner: int32 [16, 8, 1024, 1], P('gx', 'gy'), may hold values from 0 to 127; in each aligned block of 1024 rows (0 to 1023, 1024 to 2047, ..., all dimensions but the last counted through in order) at most 16 rows name the same one
Outputs:
- moved_bricks: float32 [128, 128, 16, 256], P(('gx', 'gy'))
The draws below stay inside these ranges and needn't reach their ends.
Inputs may be any that keep to these rules, and one draw needn't show every extreme that they name: `stoichiometry`: every row has one nonzero entry, +1 or -1; every species is raised by exactly one reaction and lowered by exactly one. extent[d] lies from 12 below to 5 below the lattice's cells along species d (16, 1024, 64, 32). `slab_width`: at least one entry equals 4. `new_owner`: among the 1024 bricks of one device, at most 16 have the same new owner.
All inputs are finite; a program needn't handle non-finite values.
Results may differ from the reference program's by a relative error of at most 0.000073.
Values sent between devices are 32-bit elements; how exact they have to be, the bound alone decides.
A program may use at most 128 MiB of HBM per device.

```python
import math
import jax
import jax.numpy as jnp
import numpy as np
from jax import lax

C1 = 16
C2 = 64
C3 = 8
N4 = 32
REACTIONS = 8
G2 = 16
N1 = 16
N2 = 1024
N3 = 64
MOST = 16
N_GX = 16
N_GY = 8
DEVICES = 128


def draw_stoichiometry(key, part):
    role_ids = jax.random.permutation(jax.random.fold_in(key, 37), REACTIONS)
    species = role_ids % 4
    sign_of = jnp.where(role_ids < 4, 1, -1).astype(jnp.int32)
    return (jnp.arange(4, dtype=jnp.int32)[None, :] == species[:, None]).astype(jnp.int32) * sign_of[:, None]


def draw_extent(key, part):
    lattice = jnp.array([N1, N2, N3, N4], dtype=jnp.int32)
    offsets = jax.random.randint(jax.random.fold_in(key, 11), (4,), 0, 8)
    return (lattice - 12 + offsets).astype(jnp.int32)


def draw_slab_width(key, part):
    widths = jax.random.randint(jax.random.fold_in(key, 23), (4,), 1, 5)
    chosen = jax.random.randint(jax.random.fold_in(key, 29), (), 0, 4)
    return jnp.where(jnp.arange(4) == chosen, 4, widths).astype(jnp.int32)


def steps_of(rng, shape, cuts, smallest, largest):
    factor_of, own = 1.0, jax.random.fold_in(rng, 6)
    for position, shards_of in cuts:
        draws = jnp.exp(jax.random.uniform(jax.random.fold_in(own, position), (shards_of,), jnp.float32, smallest / len(cuts), largest / len(cuts)))
        factor_of = factor_of * jnp.repeat(draws, shape[position] // shards_of).reshape([-1 if axis == position else 1 for axis in range(len(shape))])
    return factor_of


def shared_out(stream_key, own, number, rows, amount, top, most, lean):
    order = jax.random.permutation(stream_key, amount)
    packed, ordinary = shares(amount, rows * top, most, lean, True), shares(amount, rows * top, most, lean, False)
    places = jnp.arange(amount)

    def named(lengths, rotation):
        used = int((lengths > 0).sum())
        fixed = max(1, used // 4)
        moved = fixed + (places - fixed + rotation * (used - fixed)) % max(1, amount - fixed)
        return jnp.zeros((amount,), jnp.int32).at[order[jnp.where(places < fixed, places, moved)]].set(jnp.asarray(lengths, jnp.int32))

    lengths = jnp.where(number % 4 == 0, named(packed, number // 4), named(ordinary, number - number // 4 - 1))
    mixed = jax.random.permutation(jax.random.fold_in(own, 3), amount)
    source_of, receiver = mixed[0:amount // 2 * 2:2], mixed[1:amount // 2 * 2:2]
    slack = jnp.minimum(lengths[source_of] - 1, most - lengths[receiver]) // 2
    slack = jnp.where((source_of == order[0]) | (receiver == order[0]) | (lengths[receiver] == 0), 0, jnp.maximum(slack, 0))
    moved = jax.random.randint(jax.random.fold_in(own, 4), (amount // 2,), 0, 1 << 20) % (slack + 1)
    lengths = lengths.at[source_of].add(-moved).at[receiver].add(moved)
    items = jnp.searchsorted(jnp.cumsum(lengths), jnp.arange(rows * top), side="right").astype(jnp.int32)
    table = items.reshape(top, rows).T
    table = table[jax.random.permutation(jax.random.fold_in(own, 1), rows)]
    rotation = jax.random.randint(jax.random.fold_in(own, 2), (rows, 1), 0, top)
    return jnp.take_along_axis(table, (jnp.arange(top)[None, :] + rotation) % top, axis=1)


def shares(amount, total, limit, skew, full):
    loads = [(1 << 20) // math.isqrt(grade ** skew) + 1 for grade in range(1, amount + 1)]
    largest = limit if full else min(limit, max(-(-total // amount), total * loads[0] // sum(loads)))
    least = 1 if total - largest >= amount - 1 else 0
    given, surplus = [largest] + [least] * (amount - 1), total - largest - least * (amount - 1)
    while surplus > 0:
        free = [i for i in range(1, amount) if given[i] < largest] or [i for i in range(1, amount) if given[i] < limit]
        whole, left = sum([loads[i] for i in free]), surplus
        for i in free:
            extra = min(limit - given[i], max(1, left * loads[i] // whole), surplus)
            given[i] = given[i] + extra
            surplus = surplus - extra
    return np.array(given)


def setup_inputs(seed: int = 0) -> dict:
    key_of = jax.random.split(jax.random.key(seed), 8)
    probability = jnp.clip(1.0 * jax.random.uniform(key_of[0], (N_GX, C1, C2, N3 * N4), jnp.float32) ** steps_of(key_of[0], (N_GX, C1, C2, N3 * N4), ((0, 16), (3, 8)), -0.2, 0.2), 0.0, 1.0)
    extent = draw_extent(jax.random.fold_in(key_of[7], 71), 0)
    slab_width = draw_slab_width(jax.random.fold_in(key_of[7], 71), 0)
    rate_const = jnp.clip(jnp.exp(jax.random.uniform(key_of[3], (REACTIONS,), jnp.float32, math.log(0.25), math.log(1.5))), 0.25, 1.5)
    hill_const = jnp.clip(jnp.exp(jax.random.uniform(key_of[4], (REACTIONS,), jnp.float32, math.log(0.1), math.log(1.0))), 0.1, 1.0)
    stoichiometry = draw_stoichiometry(jax.random.fold_in(key_of[7], 71), 0)
    new_owner_keys = jax.random.split(jax.random.fold_in(key_of[6], 1), N_GX * N_GY * (C1 * C2) // (C1 * C2))
    new_owner_turns = jax.random.permutation(jax.random.fold_in(key_of[6], 3), N_GX * N_GY * (C1 * C2) // (C1 * C2))
    new_owner = jax.vmap(lambda own, number: shared_out(jax.random.fold_in(key_of[6], 2), own, number, C1 * C2, DEVICES, 1, MOST, 2))(new_owner_keys, new_owner_turns).reshape((N_GX, N_GY, C1 * C2, 1))
    return dict(probability=probability, extent=extent, slab_width=slab_width, rate_const=rate_const, hill_const=hill_const, stoichiometry=stoichiometry, new_owner=new_owner)


time_step = 0.15


def from_lower(values, axis_id):
    padding = [(0, 0)] * 4
    padding[axis_id] = (1, 0)
    padded = jnp.pad(values, padding)
    return lax.slice_in_dim(padded, 0, values.shape[axis_id], axis=axis_id)


def from_upper(values, axis_id):
    padding = [(0, 0)] * 4
    padding[axis_id] = (0, 1)
    padded = jnp.pad(values, padding)
    return lax.slice_in_dim(padded, 1, values.shape[axis_id] + 1, axis=axis_id)


def reference(probability, extent, slab_width, rate_const, hill_const, stoichiometry, new_owner):
    lattice = (N1, N2, N3, N4)
    lattice_field = probability.reshape(N_GX // G2, G2, C1, C2, N3, N4).transpose(0, 2, 1, 3, 4, 5).reshape(N1, N2, N3, N4)
    counts = []
    fractions = []
    for axis_id in range(4):
        view = [1, 1, 1, 1]
        view[axis_id] = lattice[axis_id]
        count_axis = jnp.arange(lattice[axis_id], dtype=jnp.int32).reshape(view)
        counts.append(count_axis)
        fractions.append(count_axis.astype(jnp.float32) / lattice[axis_id])
    inside_old = jnp.ones(lattice, bool)
    inside_new = jnp.ones(lattice, bool)
    for axis_id in range(4):
        inside_old = inside_old & (counts[axis_id] < extent[axis_id])
        inside_new = inside_new & (counts[axis_id] < extent[axis_id] + slab_width[axis_id])
    inside_old = inside_old.astype(jnp.float32)
    inside_new = inside_new.astype(jnp.float32)
    species_of = jnp.sum(jnp.abs(stoichiometry) * jnp.arange(4, dtype=jnp.int32)[None, :], axis=1)
    sign_of = jnp.sum(stoichiometry, axis=1)

    def pick_share(species_id):
        summed = jnp.zeros(lattice, jnp.float32)
        for axis_id in range(4):
            summed = summed + jnp.where(species_id == axis_id, 1.0, 0.0).astype(jnp.float32) * fractions[axis_id]
        return summed

    direction_ids = jnp.arange(8, dtype=jnp.int32)
    indicator = (stoichiometry[:, direction_ids // 2].T == (1 - 2 * (direction_ids % 2))[:, None]).astype(jnp.float32)
    direction_rates = [jnp.zeros(lattice, jnp.float32) for axis_id in range(8)]
    leave_rate = jnp.zeros(lattice, jnp.float32)
    for reaction in range(REACTIONS):
        own_share = pick_share(species_of[reaction])
        next_share = pick_share((species_of[reaction] + 1) % 4)
        scaled = next_share / hill_const[reaction]
        produce = rate_const[reaction] / (1.0 + scaled * scaled)
        degrade = 2.0 * rate_const[reaction] * own_share
        propensity = jnp.where(sign_of[reaction] > 0, produce, degrade)
        leave_rate = leave_rate + propensity
        for direction in range(8):
            direction_rates[direction] = direction_rates[direction] + indicator[direction, reaction] * propensity

    def operate(field_in):
        inflow = jnp.zeros(lattice, jnp.float32)
        for axis_id in range(4):
            inflow = inflow + from_lower(direction_rates[2 * axis_id] * field_in, axis_id)
            inflow = inflow + from_upper(direction_rates[2 * axis_id + 1] * field_in, axis_id)
        return inside_new * (inflow - leave_rate * field_in)

    initial = inside_old * lattice_field
    slope_one = operate(initial)
    slope_two = operate(initial + 0.5 * time_step * slope_one)
    slope_three = operate(initial + 0.5 * time_step * slope_two)
    slope_four = operate(initial + time_step * slope_three)
    advanced = initial + (time_step / 6.0) * (slope_one + 2.0 * slope_two + 2.0 * slope_three + slope_four)
    devices = N_GX * N_GY
    bricks = advanced.reshape(N_GX // G2, C1, G2, C2, N_GY, C3, N4).transpose(0, 2, 4, 1, 3, 5, 6).reshape(devices, C1 * C2, C3 * N4)
    owners = new_owner.reshape(devices, C1 * C2)
    one_hot = (owners[:, :, None] == jnp.arange(devices, dtype=jnp.int32)[None, None, :]).astype(jnp.int32)
    slot_rank = jnp.sum((jnp.cumsum(one_hot, axis=1) - 1) * one_hot, axis=2).astype(jnp.int32)
    senders = jnp.broadcast_to(jnp.arange(devices, dtype=jnp.int32)[:, None], owners.shape)
    moved_bricks = jnp.zeros((devices, devices, MOST, C3 * N4), jnp.float32).at[owners, senders, slot_rank].set(bricks)
    return moved_bricks
```

```python
import functools

import jax
import jax.numpy as jnp
from jax import lax
from jax.experimental import pallas as pl
from jax.experimental.pallas import tpu as pltpu
from jax.sharding import PartitionSpec as P

MESH = pl.DeviceIdType.MESH
F32 = jnp.float32
BF16 = jnp.bfloat16

time_step = 0.15
GX, GY, DEVICES = 16, 8, 128
LATTICE = (16, 1024, 64, 32)
N0, ROWS, PLANES, N4 = 16, 64, 8, 32
LANES = 128
SLOTS = 16
OLD0 = 11
PAD = 8
ALL = ROWS + 2 * PAD
FIRST = 4
GROUPS = 9
BLOCK = 512


def advance(
    params, owner, prob, row_low, row_high, plane_low, plane_high, corner_low, corner_high, sent,
    u0, u1, u2, u3, xb, onehot, prefix, ones,
    t_r0, t_f1, t_r1, t_d, t_r2, t_f2, t_f3, t_n, t_mask, target,
):
    gx = lax.axis_index("gx")
    gy = lax.axis_index("gy")

    extent = [params[d] for d in range(4)]
    edge = [params[d] + params[4 + d] for d in range(4)]

    def pick(start, species, sign):
        total = jnp.float32(0.0)
        for r in range(8):
            total = total + jnp.where(params[24 + 8 * species + r] == sign, params[start + r], jnp.float32(0.0))
        return total

    rise_rate = [pick(8, d, 1.0) for d in range(4)]
    rise_hill = [pick(16, d, 1.0) for d in range(4)]
    fall_rate = [pick(8, d, -1.0) for d in range(4)]

    def rise(d, x):
        scaled = x / jnp.full(x.shape, rise_hill[d])
        return jnp.full(x.shape, rise_rate[d]) / (1.0 + scaled * scaled)

    def fall(d, x):
        return (2.0 * fall_rate[d]) * x

    def frac(n, d):
        return n.astype(F32) * (1.0 / LATTICE[d])

    steps = [time_step / j for j in (4.0, 3.0, 2.0, 1.0)]

    n1 = (gx * ROWS - PAD + LATTICE[1] + lax.broadcasted_iota(jnp.int32, (ALL, LANES), 0)) & (LATTICE[1] - 1)
    rise_0 = rise(0, frac(n1, 1))
    leave_1 = rise_0 + fall(1, frac(n1, 1))
    fall_1 = fall(1, frac((n1 + 1) & (LATTICE[1] - 1), 1))
    in_1 = jnp.where(n1.astype(F32) < edge[1], 1.0, 0.0)
    for q in range(4):
        t_r0[q] = steps[q] * rise_0
        t_f1[q] = steps[q] * fall_1
    lane8 = lax.broadcasted_iota(jnp.int32, (8, LANES), 1)
    n3 = lane8 & (N4 - 1)
    rise_2 = rise(2, frac(n3, 3))
    leave_3 = rise_2 + fall(3, frac(n3, 3))
    fall_3 = fall(3, frac((n3 + 1) & (N4 - 1), 3))
    in_3 = jnp.where(n3.astype(F32) < edge[3], 1.0, 0.0)
    for q in range(4):
        t_f3[q] = steps[q] * fall_3
    for t in range(4):
        n2 = (gy * PLANES + 4 * (t - 1) + LATTICE[2] + (lane8 >> 5)) & (LATTICE[2] - 1)
        rise_1 = rise(1, frac(n2, 2))
        leave_23 = leave_3 + rise_1 + fall(2, frac(n2, 2))
        fall_2 = fall(2, frac((n2 + 1) & (LATTICE[2] - 1), 2))
        in_2 = jnp.where(n2.astype(F32) < edge[2], 1.0, 0.0)
        old_23 = (n2.astype(F32) < extent[2]) & (n3.astype(F32) < extent[3])
        old_1 = n1.astype(F32) < extent[1]
        t_mask[t] = jnp.where(
            old_1 & jnp.concatenate([old_23] * (ALL // 8), axis=0), extent[0], 0.0
        )
        rise_1 = jnp.concatenate([rise_1] * (ALL // 8), axis=0)
        leave_23 = jnp.concatenate([leave_23] * (ALL // 8), axis=0)
        for q in range(4):
            t_r2[q, t] = steps[q] * (rise_2 * in_2)
            t_f2[q, t] = steps[q] * fall_2
            t_r1[q, t] = steps[q] * (rise_1 * in_1)
            t_d[q, t] = (-steps[q]) * (leave_1 + leave_23)

    def species_zero(n0, _):
        here = jnp.full((8, LANES), n0, jnp.int32)
        rise_3 = rise(3, frac(here, 0))
        leave_0 = rise_3 + fall(0, frac(here, 0))
        fall_0 = fall(0, frac(here + 1, 0))
        in_0 = jnp.where(here.astype(F32) < edge[0], 1.0, 0.0)
        for q in range(4):
            t_n[q, n0, 0] = steps[q] * (rise_3 * in_3)
            t_n[q, n0, 1] = steps[q] * fall_0
            t_n[q, n0, 2] = (-steps[q]) * leave_0
            t_n[q, n0, 3] = in_0
        return 0

    lax.fori_loop(0, N0 - 1, species_zero, 0)

    zero = jnp.zeros((ALL, LANES), F32)
    for t in range(4):
        for u, ks in (
            (u0, (0, 12, 13, 14, 15, 16)), (u1, (0, 13, 14)), (u2, (0, 14, 15)), (u3, (0, 15, 16))
        ):
            for k in ks:
                u[t, k] = zero
    xb[pl.ds((N0 - 1) * ROWS, ROWS), :] = jnp.zeros((ROWS, 4 * LANES), BF16)

    prefix[...] = jnp.where(
        lax.broadcasted_iota(jnp.int32, (128, 128), 0) < lax.broadcasted_iota(jnp.int32, (128, 128), 1), 1.0, 0.0
    ).astype(BF16)
    ones[...] = jnp.ones((128, 128), BF16)
    running = jnp.zeros((DEVICES, 128), F32)
    peer = lax.broadcasted_iota(jnp.int32, (DEVICES, 128), 0)
    for b in range(8):
        part = owner[:, pl.ds(b * 128, 128)]
        hit = jnp.where(peer == part, 1.0, 0.0)
        hit16 = hit.astype(BF16)
        count = running + jnp.dot(hit16, prefix[...], preferred_element_type=F32)
        running = running + jnp.dot(hit16, ones[...], preferred_element_type=F32)
        rank = jnp.sum(hit * count, axis=0, keepdims=True)
        target[:, pl.ds(b * 128, 128)] = part.astype(F32) * float(SLOTS) + rank

    def one_hot(i, _):
        row = lax.broadcasted_iota(jnp.int32, (32, 1024), 0) + i * 32
        onehot[pl.ds(pl.multiple_of(i * 32, 32), 32), :] = jnp.where(
            row.astype(F32) == target[...], 1.0, 0.0
        ).astype(BF16)
        return 0

    lax.fori_loop(0, DEVICES * SLOTS // 32, one_hot, 0)

    def prepare(n0, _):
        def put(t, row, count, values):
            rows = pl.ds(row, count)
            u0[t, n0 + 1, rows, :] = jnp.where(n0.astype(F32) < t_mask[t, rows, :], values, 0.0)

        for h in range(2):
            lanes = pl.ds(h * LANES, LANES)
            put(1 + h, 0, PAD, row_low[n0, :, lanes])
            put(1 + h, PAD + ROWS, PAD, row_high[n0, :, lanes])
            put(1 + h, PAD, ROWS, prob[n0, :, lanes])
        for t, plane, corner in ((0, plane_low, corner_low), (3, plane_high, corner_high)):
            put(t, PAD, ROWS, plane[n0])
            put(t, 0, PAD, corner[n0])
            put(t, PAD + ROWS, 4, corner[n0, pl.ds(0, 4), :])
        return 0

    lax.fori_loop(0, OLD0, prepare, 0)

    lane = lax.broadcasted_iota(jnp.int32, (8, LANES), 1)
    first_plane = lane < N4
    last_plane = lane >= LANES - N4

    def stage(q, src, dst):
        last = q == 3

        def body(n0, _):
            r3, f0, l0, m0 = (t_n[q, n0, i] for i in range(4))
            kept = {1: [], 2: []}
            for g in range(8 if last else GROUPS):
                row = 8 * g + (PAD if last else FIRST)
                rows = pl.ds(row, 8)
                r0 = t_r0[q, rows, :] * m0
                f1 = t_f1[q, rows, :]
                centre = [src[a, n0 + 1, rows, :] for a in range(4)]
                up = [pltpu.roll(c, N4, 1) for c in centre]
                down = [pltpu.roll(c, LANES - N4, 1) for c in centre]
                for a in ((1, 2) if last else range(4)):
                    c = centre[a]
                    from_below = jnp.where(first_plane, up[a - 1], up[a]) if a > 0 else up[a]
                    from_above = jnp.where(last_plane, down[a + 1], down[a]) if a < 3 else down[a]
                    acc = u0[a, n0 + 1, rows, :] + (t_d[q, a, rows, :] + l0) * c
                    acc = acc + (r0 * src[a, n0, rows, :] + f0 * src[a, n0 + 2, rows, :])
                    acc = acc + (
                        t_r1[q, a, rows, :] * src[a, n0 + 1, pl.ds(row - 1, 8), :]
                        + f1 * src[a, n0 + 1, pl.ds(row + 1, 8), :]
                    )
                    acc = acc + (t_r2[q, a] * from_below + t_f2[q, a] * from_above)
                    acc = acc + (r3 * pltpu.roll(c, 1, 1) + t_f3[q] * pltpu.roll(c, LANES - 1, 1))
                    if last:
                        kept[a].append(acc)
                    else:
                        dst[a, n0 + 1, rows, :] = acc
                if last and g % 2 == 1:
                    place = pl.ds(pl.multiple_of(n0 * ROWS + 8 * (g - 1), 16), 16)
                    for a in (1, 2):
                        pair = jnp.concatenate(kept[a], axis=0)
                        kept[a] = []
                        high = pair.astype(BF16)
                        low = (pair - high.astype(F32)).astype(BF16)
                        dst[place, pl.ds((a - 1) * LANES, LANES)] = high
                        dst[place, pl.ds((a + 1) * LANES, LANES)] = low
            return 0

        lax.fori_loop(0, 12 + q, body, 0)

    stage(0, u0, u1)
    stage(1, u1, u2)
    stage(2, u2, u3)
    stage(3, u3, xb)

    def permute(i, _):
        place = pl.ds(pl.multiple_of(i * BLOCK, BLOCK), BLOCK)
        both = jnp.dot(onehot[place, :], xb[...], preferred_element_type=F32)
        sent[place, :] = both[:, :2 * LANES] + both[:, 2 * LANES:]
        return 0

    lax.fori_loop(0, DEVICES * SLOTS // BLOCK, permute, 0)


def ring(values, axis, shift):
    count = lax.axis_size(axis)
    return lax.ppermute(values, axis, [(i, (i + shift) % count) for i in range(count)])


def shards(probability, extent, slab_width, rate_const, hill_const, stoichiometry, new_owner):
    vmem = pltpu.VMEM
    field = probability[0]
    inner = field[:OLD0]
    row_low = ring(inner[:, ROWS - PAD:], "gx", 1)
    row_high = ring(inner[:, :PAD], "gx", -1)
    plane_low = ring(inner[:, :, LANES:], "gy", 1)
    plane_high = ring(inner[:, :, :LANES], "gy", -1)
    corner = jnp.concatenate([row_high[:, :4], row_low[:, 4:]], axis=1)
    corner_low = ring(corner[:, :, LANES:], "gy", 1)
    corner_high = ring(corner[:, :, :LANES], "gy", -1)
    params = jnp.concatenate(
        [extent.astype(F32), slab_width.astype(F32), rate_const, hill_const, stoichiometry.T.reshape(32).astype(F32)]
    )
    whole = pl.BlockSpec(memory_space=pltpu.VMEM)
    sent = pl.pallas_call(
        advance,
        out_shape=jax.ShapeDtypeStruct((DEVICES * SLOTS, PLANES * N4), F32),
        in_specs=[pl.BlockSpec(memory_space=pltpu.SMEM)] + [whole] * 8,
        out_specs=whole,
        scratch_shapes=[
            vmem((4, N0 + 1, ALL, LANES), F32),
            vmem((4, N0 + 1, ALL, LANES), F32),
            vmem((4, N0 + 1, ALL, LANES), F32),
            vmem((4, N0 + 1, ALL, LANES), F32),
            vmem((N0 * ROWS, 4 * LANES), BF16),
            vmem((DEVICES * SLOTS, N0 * ROWS), BF16),
            vmem((128, 128), BF16),
            vmem((128, 128), BF16),
            vmem((4, ALL, LANES), F32),
            vmem((4, ALL, LANES), F32),
            vmem((4, 4, ALL, LANES), F32),
            vmem((4, 4, ALL, LANES), F32),
            vmem((4, 4, 8, LANES), F32),
            vmem((4, 4, 8, LANES), F32),
            vmem((4, 8, LANES), F32),
            vmem((4, N0, 4, 8, LANES), F32),
            vmem((4, ALL, LANES), F32),
            vmem((1, N0 * ROWS), F32),
        ],
        compiler_params=pltpu.CompilerParams(vmem_limit_bytes=40 * 1024 * 1024),
        name="advance",
    )(
        params, new_owner.reshape(1, N0 * ROWS), field, row_low, row_high, plane_low, plane_high,
        corner_low, corner_high,
    )
    moved = lax.all_to_all(
        sent.reshape(DEVICES, SLOTS, PLANES * N4), ("gx", "gy"), split_axis=0, concat_axis=0, tiled=True
    )
    return moved[None]


def solution(mesh):
    in_specs = (P("gx", None, None, "gy"), P(), P(), P(), P(), P(), P("gx", "gy", None, None))
    out_specs = P(("gx", "gy"), None, None, None)
    return jax.shard_map(shards, mesh=mesh, in_specs=in_specs, out_specs=out_specs, check_vma=False)
```

```python
import functools

import jax
import jax.numpy as jnp
from jax import lax
from jax.experimental import pallas as pl
from jax.experimental.pallas import tpu as pltpu
from jax.sharding import PartitionSpec as P

MESH = pl.DeviceIdType.MESH
F32 = jnp.float32
BF16 = jnp.bfloat16

time_step = 0.15
GX, GY, DEVICES = 16, 8, 128
LATTICE = (16, 1024, 64, 32)
N0, ROWS, PLANES, N4 = 16, 64, 8, 32
LANES = 128
SLOTS = 16
OLD0 = 11
FACE = 8
REACH = 4
FIRST = 8
OWN = FIRST + REACH
GROUPS = 9
WORK = 8 * GROUPS
ALL = WORK + 2 * FIRST
BLOCK = 512


def advance(
    params, owner, prob, row_low, row_high, plane_low, plane_high, corner_low, corner_high, sent,
    u0, u1, u2, u3, xb, onehot, prefix, ones,
    t_r0, t_f1, t_r1, t_d, t_r2, t_f2, t_f3, t_n, t_mask, target, by_one, even, odd,
):
    gx = lax.axis_index("gx")
    gy = lax.axis_index("gy")

    extent = [params[d] for d in range(4)]
    edge = [params[d] + params[4 + d] for d in range(4)]

    def pick(start, species, sign):
        total = jnp.float32(0.0)
        for r in range(8):
            total = total + jnp.where(params[24 + 8 * species + r] == sign, params[start + r], jnp.float32(0.0))
        return total

    rise_rate = [pick(8, d, 1.0) for d in range(4)]
    rise_hill = [pick(16, d, 1.0) for d in range(4)]
    fall_rate = [pick(8, d, -1.0) for d in range(4)]

    def rise(d, x):
        scaled = x / jnp.full(x.shape, rise_hill[d])
        return jnp.full(x.shape, rise_rate[d]) / (1.0 + scaled * scaled)

    def fall(d, x):
        return (2.0 * fall_rate[d]) * x

    def frac(n, d):
        return n.astype(F32) * (1.0 / LATTICE[d])

    steps = [time_step / j for j in (4.0, 3.0, 2.0, 1.0)]

    n1 = (gx * ROWS - OWN + LATTICE[1] + lax.broadcasted_iota(jnp.int32, (ALL, LANES), 0)) & (LATTICE[1] - 1)
    rise_0 = rise(0, frac(n1, 1))
    leave_1 = rise_0 + fall(1, frac(n1, 1))
    fall_1 = fall(1, frac((n1 + 1) & (LATTICE[1] - 1), 1))
    in_1 = jnp.where(n1.astype(F32) < edge[1], 1.0, 0.0)
    for q in range(4):
        t_r0[q] = steps[q] * rise_0
        t_f1[q] = steps[q] * fall_1
    lane8 = lax.broadcasted_iota(jnp.int32, (8, LANES), 1)
    n3 = lane8 & (N4 - 1)
    rise_2 = rise(2, frac(n3, 3))
    leave_3 = rise_2 + fall(3, frac(n3, 3))
    fall_3 = fall(3, frac((n3 + 1) & (N4 - 1), 3))
    in_3 = jnp.where(n3.astype(F32) < edge[3], 1.0, 0.0)
    for q in range(4):
        t_f3[q] = steps[q] * fall_3
    for t in range(4):
        n2 = (gy * PLANES + 4 * (t - 1) + LATTICE[2] + (lane8 >> 5)) & (LATTICE[2] - 1)
        rise_1 = rise(1, frac(n2, 2))
        leave_23 = leave_3 + rise_1 + fall(2, frac(n2, 2))
        fall_2 = fall(2, frac((n2 + 1) & (LATTICE[2] - 1), 2))
        in_2 = jnp.where(n2.astype(F32) < edge[2], 1.0, 0.0)
        old_23 = (n2.astype(F32) < extent[2]) & (n3.astype(F32) < extent[3])
        old_1 = n1.astype(F32) < extent[1]
        t_mask[t] = jnp.where(
            old_1 & jnp.concatenate([old_23] * (ALL // 8), axis=0), extent[0], 0.0
        )
        rise_1 = jnp.concatenate([rise_1] * (ALL // 8), axis=0)
        leave_23 = jnp.concatenate([leave_23] * (ALL // 8), axis=0)
        for q in range(4):
            t_r2[q, t] = steps[q] * (rise_2 * in_2)
            t_f2[q, t] = steps[q] * fall_2
            t_r1[q, t] = steps[q] * (rise_1 * in_1)
            t_d[q, t] = (-steps[q]) * (leave_1 + leave_23)

    def species_zero(n0, _):
        here = jnp.full((8, LANES), n0, jnp.int32)
        rise_3 = rise(3, frac(here, 0))
        leave_0 = rise_3 + fall(0, frac(here, 0))
        fall_0 = fall(0, frac(here + 1, 0))
        in_0 = jnp.where(here.astype(F32) < edge[0], 1.0, 0.0)
        for q in range(4):
            t_n[q, n0, 0] = steps[q] * (rise_3 * in_3)
            t_n[q, n0, 1] = steps[q] * fall_0
            t_n[q, n0, 2] = (-steps[q]) * leave_0
            t_n[q, n0, 3] = in_0
        return 0

    lax.fori_loop(0, N0, species_zero, 0)

    zero = jnp.zeros((ALL, LANES), F32)
    for t in range(4):
        for u, ks in (
            (u0, (0, 12, 13, 14, 15, 16)), (u1, (0, 13, 14, 15)), (u2, (0, 15)), (u3, (0, 15, 16, 17))
        ):
            for k in ks:
                u[t, k] = zero
    prefix[...] = jnp.where(
        lax.broadcasted_iota(jnp.int32, (128, 128), 0) < lax.broadcasted_iota(jnp.int32, (128, 128), 1), 1.0, 0.0
    ).astype(BF16)
    ones[...] = jnp.ones((128, 128), BF16)
    running = jnp.zeros((DEVICES, 128), F32)
    ranks = []
    peer = lax.broadcasted_iota(jnp.int32, (DEVICES, 128), 0)
    for b in range(8):
        part = owner[:, pl.ds(b * 128, 128)]
        hit = jnp.where(peer == part, 1.0, 0.0)
        hit16 = hit.astype(BF16)
        count = running + jnp.dot(hit16, prefix[...], preferred_element_type=F32)
        running = running + jnp.dot(hit16, ones[...], preferred_element_type=F32)
        rank = jnp.sum(hit * count, axis=0, keepdims=True)
        ranks.append(rank)

    slot = lax.broadcasted_iota(jnp.int32, (SLOTS, 1024), 0).astype(F32)
    at_slot = jnp.where(slot == jnp.concatenate(ranks, axis=1), 1.0, 0.0).astype(BF16)
    owners = jnp.broadcast_to(owner[...].astype(F32), (SLOTS, 1024)).astype(BF16)

    def one_hot(o, now):
        onehot[pl.ds(pl.multiple_of(o * SLOTS, SLOTS), SLOTS), :] = jnp.where(
            owners == now, at_slot, jnp.zeros_like(at_slot)
        )
        return now + jnp.ones_like(now)

    lax.fori_loop(0, DEVICES, one_hot, jnp.zeros((SLOTS, 1024), BF16))

    source = lax.broadcasted_iota(jnp.int32, (2 * LANES, 2 * LANES), 0) & (LANES - 1)
    column = lax.broadcasted_iota(jnp.int32, (2 * LANES, 2 * LANES), 1)
    wanted = jnp.where(column < LANES, column + LANES - 1, column + 1) & (LANES - 1)
    by_one[...] = jnp.where(source == wanted, 1.0, 0.0).astype(BF16)

    def prepare(n0, _):
        def put(t, row, count, values):
            rows = pl.ds(row, count)
            u0[t, n0 + 1, rows, :] = jnp.where(n0.astype(F32) < t_mask[t, rows, :], values, 0.0)

        for h in range(2):
            lanes = pl.ds(h * LANES, LANES)
            put(1 + h, FIRST, REACH, row_low[n0, pl.ds(FACE - REACH, REACH), lanes])
            put(1 + h, OWN + ROWS, REACH, row_high[n0, pl.ds(0, REACH), lanes])
            put(1 + h, OWN, ROWS, prob[n0, :, lanes])
        for t, plane, corner in ((0, plane_low, corner_low), (3, plane_high, corner_high)):
            put(t, FIRST, REACH, corner[n0, pl.ds(REACH, REACH), :])
            put(t, OWN + ROWS, REACH, corner[n0, pl.ds(0, REACH), :])
            put(t, OWN, ROWS, plane[n0])
        return 0

    lax.fori_loop(0, OLD0, prepare, 0)

    lane = lax.broadcasted_iota(jnp.int32, (8, LANES), 1)
    first_plane = lane < N4
    last_plane = lane >= LANES - N4

    def shift(q, src, n0, moved):
        tiles = (1, 2) if q == 3 else range(4)
        rows = jnp.concatenate([src[a, n0 + 1, pl.ds(FIRST, WORK), :] for a in tiles], axis=0)
        high = rows.astype(BF16)
        low = (rows - high.astype(F32)).astype(BF16)
        both = jnp.dot(jnp.concatenate([high, low], axis=1), by_one[...], preferred_element_type=F32)
        count = pl.ds(0, rows.shape[0])
        moved[0, count, :] = both[:, :LANES]
        moved[1, count, :] = both[:, LANES:]

    def stage(q, src, dst):
        last = q == 3

        def update(n0, moved):
            r3, f0, l0, m0 = (t_n[q, n0, i] for i in range(4))
            kept = {1: [], 2: []}
            for g in range(8 if last else GROUPS):
                row = 8 * g + (OWN if last else FIRST)
                rows = pl.ds(row, 8)
                r0 = t_r0[q, rows, :] * m0
                f1 = t_f1[q, rows, :]
                centre = [src[a, n0 + 1, rows, :] for a in range(4)]
                up = [pltpu.roll(c, N4, 1) for c in centre]
                down = [pltpu.roll(c, LANES - N4, 1) for c in centre]
                for a in ((1, 2) if last else range(4)):
                    c = centre[a]
                    from_below = jnp.where(first_plane, up[a - 1], up[a]) if a > 0 else up[a]
                    from_above = jnp.where(last_plane, down[a + 1], down[a]) if a < 3 else down[a]
                    acc = u0[a, n0 + 1, rows, :] + (t_d[q, a, rows, :] + l0) * c
                    acc = acc + (r0 * src[a, n0, rows, :] + f0 * src[a, n0 + 2, rows, :])
                    acc = acc + (
                        t_r1[q, a, rows, :] * src[a, n0 + 1, pl.ds(row - 1, 8), :]
                        + f1 * src[a, n0 + 1, pl.ds(row + 1, 8), :]
                    )
                    acc = acc + (t_r2[q, a] * from_below + t_f2[q, a] * from_above)
                    place = pl.ds(WORK * (a - 1 if last else a) + row - FIRST, 8)
                    acc = acc + (r3 * moved[0, place, :] + t_f3[q] * moved[1, place, :])
                    if last:
                        kept[a].append(acc)
                    else:
                        dst[a, n0 + 1, rows, :] = acc
                if last and g % 2 == 1:
                    place = pl.ds(pl.multiple_of(n0 * ROWS + 8 * (g - 1), 16), 16)
                    for a in (1, 2):
                        pair = jnp.concatenate(kept[a], axis=0)
                        kept[a] = []
                        high = pair.astype(BF16)
                        low = (pair - high.astype(F32)).astype(BF16)
                        dst[place, pl.ds((a - 1) * LANES, LANES)] = high
                        dst[place, pl.ds((a + 1) * LANES, LANES)] = low

        def body(i, _):
            n0 = 2 * i
            shift(q, src, n0 + 1, odd)
            update(n0, even)
            shift(q, src, n0 + 2, even)
            update(n0 + 1, odd)
            return 0

        shift(q, src, 0, even)
        lax.fori_loop(0, (13 + q) // 2, body, 0)

    stage(0, u0, u1)
    stage(1, u1, u2)
    stage(2, u2, u3)
    stage(3, u3, xb)

    def permute(i, _):
        place = pl.ds(pl.multiple_of(i * BLOCK, BLOCK), BLOCK)
        both = jnp.dot(onehot[place, :], xb[...], preferred_element_type=F32)
        sent[place, :] = both[:, :2 * LANES] + both[:, 2 * LANES:]
        return 0

    lax.fori_loop(0, DEVICES * SLOTS // BLOCK, permute, 0)


def ring(values, axis, shift):
    count = lax.axis_size(axis)
    return lax.ppermute(values, axis, [(i, (i + shift) % count) for i in range(count)])


def shards(probability, extent, slab_width, rate_const, hill_const, stoichiometry, new_owner):
    vmem = pltpu.VMEM
    field = probability[0]
    inner = field[:OLD0]
    row_low = ring(inner[:, ROWS - FACE:], "gx", 1)
    row_high = ring(inner[:, :FACE], "gx", -1)
    plane_low = ring(inner[:, :, LANES:], "gy", 1)
    plane_high = ring(inner[:, :, :LANES], "gy", -1)
    corner = jnp.concatenate([row_high[:, :4], row_low[:, 4:]], axis=1)
    corner_low = ring(corner[:, :, LANES:], "gy", 1)
    corner_high = ring(corner[:, :, :LANES], "gy", -1)
    params = jnp.concatenate(
        [extent.astype(F32), slab_width.astype(F32), rate_const, hill_const, stoichiometry.T.reshape(32).astype(F32)]
    )
    whole = pl.BlockSpec(memory_space=pltpu.VMEM)
    sent = pl.pallas_call(
        advance,
        out_shape=jax.ShapeDtypeStruct((DEVICES * SLOTS, PLANES * N4), F32),
        in_specs=[pl.BlockSpec(memory_space=pltpu.SMEM)] + [whole] * 8,
        out_specs=whole,
        scratch_shapes=[
            vmem((4, N0 + 2, ALL, LANES), F32),
            vmem((4, N0 + 2, ALL, LANES), F32),
            vmem((4, N0 + 2, ALL, LANES), F32),
            vmem((4, N0 + 2, ALL, LANES), F32),
            vmem((N0 * ROWS, 4 * LANES), BF16),
            vmem((DEVICES * SLOTS, N0 * ROWS), BF16),
            vmem((128, 128), BF16),
            vmem((128, 128), BF16),
            vmem((4, ALL, LANES), F32),
            vmem((4, ALL, LANES), F32),
            vmem((4, 4, ALL, LANES), F32),
            vmem((4, 4, ALL, LANES), F32),
            vmem((4, 4, 8, LANES), F32),
            vmem((4, 4, 8, LANES), F32),
            vmem((4, 8, LANES), F32),
            vmem((4, N0, 4, 8, LANES), F32),
            vmem((4, ALL, LANES), F32),
            vmem((1, N0 * ROWS), F32),
            vmem((2 * LANES, 2 * LANES), BF16),
            vmem((2, 4 * WORK, LANES), F32),
            vmem((2, 4 * WORK, LANES), F32),
        ],
        compiler_params=pltpu.CompilerParams(vmem_limit_bytes=40 * 1024 * 1024),
        name="advance",
    )(
        params, new_owner.reshape(1, N0 * ROWS), field, row_low, row_high, plane_low, plane_high,
        corner_low, corner_high,
    )
    moved = lax.all_to_all(
        sent.reshape(DEVICES, SLOTS, PLANES * N4), ("gx", "gy"), split_axis=0, concat_axis=0, tiled=True
    )
    return moved[None]


def solution(mesh):
    in_specs = (P("gx", None, None, "gy"), P(), P(), P(), P(), P(), P("gx", "gy", None, None))
    out_specs = P(("gx", "gy"), None, None, None)
    return jax.shard_map(shards, mesh=mesh, in_specs=in_specs, out_specs=out_specs, check_vma=False)
```

```python
import functools

import jax
import jax.numpy as jnp
from jax import lax
from jax.experimental import pallas as pl
from jax.experimental.pallas import tpu as pltpu
from jax.sharding import PartitionSpec as P

MESH = pl.DeviceIdType.MESH
F32 = jnp.float32
BF16 = jnp.bfloat16

time_step = 0.15
GX, GY, DEVICES = 16, 8, 128
LATTICE = (16, 1024, 64, 32)
N0, ROWS, PLANES, N4 = 16, 64, 8, 32
LANES = 128
SLOTS = 16
OLD0 = 11
FACE = 8
REACH = 4
FIRST = 8
OWN = FIRST + REACH
GROUPS = 9
WORK = 8 * GROUPS
ALL = WORK + 2 * FIRST
BLOCK = 512


def prepare_tables(
    params, owner, t_r0, t_f1, t_r1, t_d, t_r2, t_f2, t_f3, t_n, t_mask, by_one, onehot, prefix, ones
):
    gx = lax.axis_index("gx")
    gy = lax.axis_index("gy")

    extent = [params[d] for d in range(4)]
    edge = [params[d] + params[4 + d] for d in range(4)]

    def pick(start, species, sign):
        total = jnp.float32(0.0)
        for r in range(8):
            total = total + jnp.where(params[24 + 8 * species + r] == sign, params[start + r], jnp.float32(0.0))
        return total

    rise_rate = [pick(8, d, 1.0) for d in range(4)]
    rise_hill = [pick(16, d, 1.0) for d in range(4)]
    fall_rate = [pick(8, d, -1.0) for d in range(4)]

    def rise(d, x):
        scaled = x / jnp.full(x.shape, rise_hill[d])
        return jnp.full(x.shape, rise_rate[d]) / (1.0 + scaled * scaled)

    def fall(d, x):
        return (2.0 * fall_rate[d]) * x

    def frac(n, d):
        return n.astype(F32) * (1.0 / LATTICE[d])

    steps = [time_step / j for j in (4.0, 3.0, 2.0, 1.0)]

    n1 = (gx * ROWS - OWN + LATTICE[1] + lax.broadcasted_iota(jnp.int32, (ALL, LANES), 0)) & (LATTICE[1] - 1)
    rise_0 = rise(0, frac(n1, 1))
    leave_1 = rise_0 + fall(1, frac(n1, 1))
    fall_1 = fall(1, frac((n1 + 1) & (LATTICE[1] - 1), 1))
    in_1 = jnp.where(n1.astype(F32) < edge[1], 1.0, 0.0)
    for q in range(4):
        t_r0[q] = steps[q] * rise_0
        t_f1[q] = steps[q] * fall_1
    lane8 = lax.broadcasted_iota(jnp.int32, (8, LANES), 1)
    n3 = lane8 & (N4 - 1)
    rise_2 = rise(2, frac(n3, 3))
    leave_3 = rise_2 + fall(3, frac(n3, 3))
    fall_3 = fall(3, frac((n3 + 1) & (N4 - 1), 3))
    in_3 = jnp.where(n3.astype(F32) < edge[3], 1.0, 0.0)
    for q in range(4):
        t_f3[q] = steps[q] * fall_3
    for t in range(4):
        n2 = (gy * PLANES + 4 * (t - 1) + LATTICE[2] + (lane8 >> 5)) & (LATTICE[2] - 1)
        rise_1 = rise(1, frac(n2, 2))
        leave_23 = leave_3 + rise_1 + fall(2, frac(n2, 2))
        fall_2 = fall(2, frac((n2 + 1) & (LATTICE[2] - 1), 2))
        in_2 = jnp.where(n2.astype(F32) < edge[2], 1.0, 0.0)
        old_23 = (n2.astype(F32) < extent[2]) & (n3.astype(F32) < extent[3])
        old_1 = n1.astype(F32) < extent[1]
        t_mask[t] = jnp.where(
            old_1 & jnp.concatenate([old_23] * (ALL // 8), axis=0), extent[0], 0.0
        )
        rise_1 = jnp.concatenate([rise_1] * (ALL // 8), axis=0)
        leave_23 = jnp.concatenate([leave_23] * (ALL // 8), axis=0)
        for q in range(4):
            t_r2[q, t] = steps[q] * (rise_2 * in_2)
            t_f2[q, t] = steps[q] * fall_2
            t_r1[q, t] = steps[q] * (rise_1 * in_1)
            t_d[q, t] = (-steps[q]) * (leave_1 + leave_23)

    def species_zero(n0, _):
        here = jnp.full((8, LANES), n0, jnp.int32)
        rise_3 = rise(3, frac(here, 0))
        leave_0 = rise_3 + fall(0, frac(here, 0))
        fall_0 = fall(0, frac(here + 1, 0))
        in_0 = jnp.where(here.astype(F32) < edge[0], 1.0, 0.0)
        for q in range(4):
            t_n[q, n0, 0] = steps[q] * (rise_3 * in_3)
            t_n[q, n0, 1] = steps[q] * fall_0
            t_n[q, n0, 2] = (-steps[q]) * leave_0
            t_n[q, n0, 3] = in_0
        return 0

    lax.fori_loop(0, N0, species_zero, 0)

    prefix[...] = jnp.where(
        lax.broadcasted_iota(jnp.int32, (128, 128), 0) < lax.broadcasted_iota(jnp.int32, (128, 128), 1), 1.0, 0.0
    ).astype(BF16)
    ones[...] = jnp.ones((128, 128), BF16)
    running = jnp.zeros((DEVICES, 128), F32)
    ranks = []
    peer = lax.broadcasted_iota(jnp.int32, (DEVICES, 128), 0)
    for b in range(8):
        part = owner[:, pl.ds(b * 128, 128)]
        hit = jnp.where(peer == part, 1.0, 0.0)
        hit16 = hit.astype(BF16)
        count = running + jnp.dot(hit16, prefix[...], preferred_element_type=F32)
        running = running + jnp.dot(hit16, ones[...], preferred_element_type=F32)
        rank = jnp.sum(hit * count, axis=0, keepdims=True)
        ranks.append(rank)

    slot = lax.broadcasted_iota(jnp.int32, (SLOTS, 1024), 0).astype(F32)
    at_slot = jnp.where(slot == jnp.concatenate(ranks, axis=1), 1.0, 0.0).astype(BF16)
    owners = jnp.broadcast_to(owner[...].astype(F32), (SLOTS, 1024)).astype(BF16)

    def one_hot(o, now):
        onehot[pl.ds(pl.multiple_of(o * SLOTS, SLOTS), SLOTS), :] = jnp.where(
            owners == now, at_slot, jnp.zeros_like(at_slot)
        )
        return now + jnp.ones_like(now)

    lax.fori_loop(0, DEVICES, one_hot, jnp.zeros((SLOTS, 1024), BF16))

    source = lax.broadcasted_iota(jnp.int32, (2 * LANES, 2 * LANES), 0) & (LANES - 1)
    column = lax.broadcasted_iota(jnp.int32, (2 * LANES, 2 * LANES), 1)
    wanted = jnp.where(column < LANES, column + LANES - 1, column + 1) & (LANES - 1)
    by_one[...] = jnp.where(source == wanted, 1.0, 0.0).astype(BF16)


def advance(
    prob, row_low, row_high, plane_low, plane_high, corner_low, corner_high,
    t_r0, t_f1, t_r1, t_d, t_r2, t_f2, t_f3, t_n, t_mask, by_one, onehot, sent,
    u0, u1, u2, u3, xb, even, odd,
):
    zero = jnp.zeros((ALL, LANES), F32)
    for t in range(4):
        for u, ks in (
            (u0, (0, 12, 13, 14, 15, 16, 17)), (u1, (0, 13, 14, 15, 16, 17)), (u2, (0, 17)), (u3, (0, 17))
        ):
            for k in ks:
                u[t, k] = zero
    def prepare(n0, _):
        def put(t, row, count, values):
            rows = pl.ds(row, count)
            u0[t, n0 + 1, rows, :] = jnp.where(n0.astype(F32) < t_mask[t, rows, :], values, 0.0)

        for h in range(2):
            lanes = pl.ds(h * LANES, LANES)
            put(1 + h, FIRST, REACH, row_low[n0, pl.ds(FACE - REACH, REACH), lanes])
            put(1 + h, OWN + ROWS, REACH, row_high[n0, pl.ds(0, REACH), lanes])
            put(1 + h, OWN, ROWS, prob[n0, :, lanes])
        for t, plane, corner in ((0, plane_low, corner_low), (3, plane_high, corner_high)):
            put(t, FIRST, REACH, corner[n0, pl.ds(REACH, REACH), :])
            put(t, OWN + ROWS, REACH, corner[n0, pl.ds(0, REACH), :])
            put(t, OWN, ROWS, plane[n0])
        return 0

    lax.fori_loop(0, OLD0, prepare, 0)

    lane = lax.broadcasted_iota(jnp.int32, (8, LANES), 1)
    first_plane = lane < N4
    last_plane = lane >= LANES - N4

    def shift(q, src, n0, moved):
        tiles = (1, 2) if q == 3 else range(4)
        f3 = t_f3[q]
        for k in range(2):
            r3 = t_n[q, n0 + k, 0]
            rows = jnp.concatenate([src[a, n0 + k + 1, pl.ds(FIRST, WORK), :] for a in tiles], axis=0)
            high = rows.astype(BF16)
            low = (rows - high.astype(F32)).astype(BF16)
            both = jnp.dot(jnp.concatenate([high, low], axis=1), by_one[...], preferred_element_type=F32)
            both = both.reshape(-1, 8, 2 * LANES)
            flow = r3[None] * both[:, :, :LANES] + f3[None] * both[:, :, LANES:]
            moved[k, pl.ds(0, rows.shape[0]), :] = flow.reshape(rows.shape)

    def stage(q, src, dst):
        last = q == 3

        def update(n0, moved):
            pair = range(2)
            f0, l0, m0 = ([t_n[q, n0 + k, i] for k in pair] for i in (1, 2, 3))
            r2 = [t_r2[q, a] for a in range(4)]
            f2 = [t_f2[q, a] for a in range(4)]
            kept = {(k, a): [] for k in pair for a in (1, 2)}
            for g in range(8 if last else GROUPS):
                row = 8 * g + (OWN if last else FIRST)
                rows = pl.ds(row, 8)
                r0 = t_r0[q, rows, :]
                f1 = t_f1[q, rows, :]
                r0 = [r0 * m0[k] for k in pair]
                centre = [[src[a, n0 + k + 1, rows, :] for a in range(4)] for k in pair]
                up = [[pltpu.roll(c, N4, 1) for c in centre[k]] for k in pair]
                down = [[pltpu.roll(c, LANES - N4, 1) for c in centre[k]] for k in pair]
                for a in ((1, 2) if last else range(4)):
                    before = [src[a, n0, rows, :], centre[0][a]]
                    after = [centre[1][a], src[a, n0 + 3, rows, :]]
                    d = t_d[q, a, rows, :]
                    r1 = t_r1[q, a, rows, :]
                    place = pl.ds(WORK * (a - 1 if last else a) + row - FIRST, 8)
                    for k in pair:
                        c = centre[k][a]
                        from_below = jnp.where(first_plane, up[k][a - 1], up[k][a]) if a > 0 else up[k][a]
                        from_above = jnp.where(last_plane, down[k][a + 1], down[k][a]) if a < 3 else down[k][a]
                        acc = u0[a, n0 + k + 1, rows, :] + (d + l0[k]) * c
                        acc = acc + (r0[k] * before[k] + f0[k] * after[k])
                        acc = acc + (
                            r1 * src[a, n0 + k + 1, pl.ds(row - 1, 8), :]
                            + f1 * src[a, n0 + k + 1, pl.ds(row + 1, 8), :]
                        )
                        acc = acc + (r2[a] * from_below + f2[a] * from_above)
                        acc = acc + moved[k, place, :]
                        if last:
                            kept[k, a].append(acc)
                        else:
                            dst[a, n0 + k + 1, rows, :] = acc
                if last and g % 2 == 1:
                    for k in pair:
                        place = pl.ds(pl.multiple_of((n0 + k) * ROWS + 8 * (g - 1), 16), 16)
                        for a in (1, 2):
                            both = jnp.concatenate(kept[k, a], axis=0)
                            kept[k, a] = []
                            high = both.astype(BF16)
                            low = (both - high.astype(F32)).astype(BF16)
                            dst[place, pl.ds((a - 1) * LANES, LANES)] = high
                            dst[place, pl.ds((a + 1) * LANES, LANES)] = low

        def body(i, _):
            n0 = 4 * i
            shift(q, src, n0 + 2, odd)
            update(n0, even)
            shift(q, src, jnp.minimum(n0 + 4, N0 - 2), even)
            update(n0 + 2, odd)
            return 0

        shift(q, src, 0, even)
        lax.fori_loop(0, 3 if q == 0 else 4, body, 0)

    stage(0, u0, u1)
    stage(1, u1, u2)
    stage(2, u2, u3)
    stage(3, u3, xb)

    def permute(i, _):
        place = pl.ds(pl.multiple_of(i * BLOCK, BLOCK), BLOCK)
        both = jnp.dot(onehot[place, :], xb[...], preferred_element_type=F32)
        sent[place, :] = both[:, :2 * LANES] + both[:, 2 * LANES:]
        return 0

    lax.fori_loop(0, DEVICES * SLOTS // BLOCK, permute, 0)


def ring(values, axis, shift):
    count = lax.axis_size(axis)
    return lax.ppermute(values, axis, [(i, (i + shift) % count) for i in range(count)])


def shards(probability, extent, slab_width, rate_const, hill_const, stoichiometry, new_owner):
    vmem = pltpu.VMEM
    field = probability[0]
    inner = field[:OLD0]
    row_low = ring(inner[:, ROWS - FACE:], "gx", 1)
    row_high = ring(inner[:, :FACE], "gx", -1)
    plane_low = ring(inner[:, :, LANES:], "gy", 1)
    plane_high = ring(inner[:, :, :LANES], "gy", -1)
    corner = jnp.concatenate([row_high[:, :4], row_low[:, 4:]], axis=1)
    corner_low = ring(corner[:, :, LANES:], "gy", 1)
    corner_high = ring(corner[:, :, :LANES], "gy", -1)
    params = jnp.concatenate(
        [extent.astype(F32), slab_width.astype(F32), rate_const, hill_const, stoichiometry.T.reshape(32).astype(F32)]
    )
    whole = pl.BlockSpec(memory_space=pltpu.VMEM)
    tables = [
        ((4, ALL, LANES), F32),
        ((4, ALL, LANES), F32),
        ((4, 4, ALL, LANES), F32),
        ((4, 4, ALL, LANES), F32),
        ((4, 4, 8, LANES), F32),
        ((4, 4, 8, LANES), F32),
        ((4, 8, LANES), F32),
        ((4, N0, 4, 8, LANES), F32),
        ((4, ALL, LANES), F32),
        ((2 * LANES, 2 * LANES), BF16),
        ((DEVICES * SLOTS, N0 * ROWS), BF16),
    ]
    made = pl.pallas_call(
        prepare_tables,
        out_shape=[jax.ShapeDtypeStruct(*table) for table in tables],
        in_specs=[pl.BlockSpec(memory_space=pltpu.SMEM), whole],
        out_specs=[whole] * len(tables),
        scratch_shapes=[vmem((128, 128), BF16), vmem((128, 128), BF16)],
        compiler_params=pltpu.CompilerParams(vmem_limit_bytes=12 * 1024 * 1024),
        cost_estimate=pl.CostEstimate(flops=10_000_000, bytes_accessed=16_000_000, transcendentals=0),
        name="prepare_tables",
    )(params, new_owner.reshape(1, N0 * ROWS))
    sent = pl.pallas_call(
        advance,
        out_shape=jax.ShapeDtypeStruct((DEVICES * SLOTS, PLANES * N4), F32),
        in_specs=[whole] * (7 + len(tables)),
        out_specs=whole,
        scratch_shapes=[
            vmem((4, N0 + 2, ALL, LANES), F32),
            vmem((4, N0 + 2, ALL, LANES), F32),
            vmem((4, N0 + 2, ALL, LANES), F32),
            vmem((4, N0 + 2, ALL, LANES), F32),
            vmem((N0 * ROWS, 4 * LANES), BF16),
            vmem((2, 4 * WORK, LANES), F32),
            vmem((2, 4 * WORK, LANES), F32),
        ],
        compiler_params=pltpu.CompilerParams(vmem_limit_bytes=32 * 1024 * 1024),
        name="advance",
    )(field, row_low, row_high, plane_low, plane_high, corner_low, corner_high, *made)
    moved = lax.all_to_all(
        sent.reshape(DEVICES, SLOTS, PLANES * N4), ("gx", "gy"), split_axis=0, concat_axis=0, tiled=True
    )
    return moved[None]


def solution(mesh):
    in_specs = (P("gx", None, None, "gy"), P(), P(), P(), P(), P(), P("gx", "gy", None, None))
    out_specs = P(("gx", "gy"), None, None, None)
    return jax.shard_map(shards, mesh=mesh, in_specs=in_specs, out_specs=out_specs, check_vma=False)
```

```python
import functools

import jax
import jax.numpy as jnp
from jax import lax
from jax.experimental import pallas as pl
from jax.experimental.pallas import tpu as pltpu
from jax.sharding import PartitionSpec as P

MESH = pl.DeviceIdType.MESH
F32 = jnp.float32
BF16 = jnp.bfloat16

time_step = 0.15
GX, GY, DEVICES = 16, 8, 128
LATTICE = (16, 1024, 64, 32)
N0, ROWS, PLANES, N4 = 16, 64, 8, 32
LANES = 128
SLOTS = 16
OLD0 = 11
FACE = 8
REACH = 4
FIRST = 8
OWN = FIRST + REACH
GROUPS = 9
WORK = 8 * GROUPS
ALL = WORK + 2 * FIRST
BLOCK = 512


def prepare_tables(
    params, owner, last_rows, first_rows, go_up, go_down, t_r0, t_f1, t_r1, t_d, t_r2, t_f2, t_f3, t_n, t_mask, by_one, onehot, prefix, ones
):
    gx = lax.axis_index("gx")
    gy = lax.axis_index("gy")

    go_up[...] = last_rows[...]
    go_down[...] = first_rows[...]

    extent = [params[d] for d in range(4)]
    edge = [params[d] + params[4 + d] for d in range(4)]

    def pick(start, species, sign):
        total = jnp.float32(0.0)
        for r in range(8):
            total = total + jnp.where(params[24 + 8 * species + r] == sign, params[start + r], jnp.float32(0.0))
        return total

    rise_rate = [pick(8, d, 1.0) for d in range(4)]
    rise_hill = [pick(16, d, 1.0) for d in range(4)]
    fall_rate = [pick(8, d, -1.0) for d in range(4)]

    def rise(d, x):
        scaled = x / jnp.full(x.shape, rise_hill[d])
        return jnp.full(x.shape, rise_rate[d]) / (1.0 + scaled * scaled)

    def fall(d, x):
        return (2.0 * fall_rate[d]) * x

    def frac(n, d):
        return n.astype(F32) * (1.0 / LATTICE[d])

    steps = [time_step / j for j in (4.0, 3.0, 2.0, 1.0)]

    n1 = (gx * ROWS - OWN + LATTICE[1] + lax.broadcasted_iota(jnp.int32, (ALL, LANES), 0)) & (LATTICE[1] - 1)
    rise_0 = rise(0, frac(n1, 1))
    leave_1 = rise_0 + fall(1, frac(n1, 1))
    fall_1 = fall(1, frac((n1 + 1) & (LATTICE[1] - 1), 1))
    in_1 = jnp.where(n1.astype(F32) < edge[1], 1.0, 0.0)
    for q in range(4):
        t_r0[q] = steps[q] * rise_0
        t_f1[q] = steps[q] * fall_1
    lane8 = lax.broadcasted_iota(jnp.int32, (8, LANES), 1)
    n3 = lane8 & (N4 - 1)
    rise_2 = rise(2, frac(n3, 3))
    leave_3 = rise_2 + fall(3, frac(n3, 3))
    fall_3 = fall(3, frac((n3 + 1) & (N4 - 1), 3))
    in_3 = jnp.where(n3.astype(F32) < edge[3], 1.0, 0.0)
    for q in range(4):
        t_f3[q] = steps[q] * fall_3
    for t in range(4):
        n2 = (gy * PLANES + 4 * (t - 1) + LATTICE[2] + (lane8 >> 5)) & (LATTICE[2] - 1)
        rise_1 = rise(1, frac(n2, 2))
        leave_23 = leave_3 + rise_1 + fall(2, frac(n2, 2))
        fall_2 = fall(2, frac((n2 + 1) & (LATTICE[2] - 1), 2))
        in_2 = jnp.where(n2.astype(F32) < edge[2], 1.0, 0.0)
        old_23 = (n2.astype(F32) < extent[2]) & (n3.astype(F32) < extent[3])
        old_1 = n1.astype(F32) < extent[1]
        t_mask[t] = jnp.where(
            old_1 & jnp.concatenate([old_23] * (ALL // 8), axis=0), extent[0], 0.0
        )
        rise_1 = jnp.concatenate([rise_1] * (ALL // 8), axis=0)
        leave_23 = jnp.concatenate([leave_23] * (ALL // 8), axis=0)
        for q in range(4):
            t_r2[q, t] = steps[q] * (rise_2 * in_2)
            t_f2[q, t] = steps[q] * fall_2
            t_r1[q, t] = steps[q] * (rise_1 * in_1)
            t_d[q, t] = (-steps[q]) * (leave_1 + leave_23)

    def species_zero(n0, _):
        here = jnp.full((8, LANES), n0, jnp.int32)
        rise_3 = rise(3, frac(here, 0))
        leave_0 = rise_3 + fall(0, frac(here, 0))
        fall_0 = fall(0, frac(here + 1, 0))
        in_0 = jnp.where(here.astype(F32) < edge[0], 1.0, 0.0)
        for q in range(4):
            t_n[q, n0, 0] = steps[q] * (rise_3 * in_3)
            t_n[q, n0, 1] = steps[q] * fall_0
            t_n[q, n0, 2] = (-steps[q]) * leave_0
            t_n[q, n0, 3] = in_0
        return 0

    lax.fori_loop(0, N0, species_zero, 0)

    prefix[...] = jnp.where(
        lax.broadcasted_iota(jnp.int32, (128, 128), 0) < lax.broadcasted_iota(jnp.int32, (128, 128), 1), 1.0, 0.0
    ).astype(BF16)
    ones[...] = jnp.ones((128, 128), BF16)
    running = jnp.zeros((DEVICES, 128), F32)
    ranks = []
    peer = lax.broadcasted_iota(jnp.int32, (DEVICES, 128), 0)
    for b in range(8):
        part = owner[:, pl.ds(b * 128, 128)]
        hit = jnp.where(peer == part, 1.0, 0.0)
        hit16 = hit.astype(BF16)
        count = running + jnp.dot(hit16, prefix[...], preferred_element_type=F32)
        running = running + jnp.dot(hit16, ones[...], preferred_element_type=F32)
        rank = jnp.sum(hit * count, axis=0, keepdims=True)
        ranks.append(rank)

    slot = lax.broadcasted_iota(jnp.int32, (SLOTS, 1024), 0).astype(F32)
    at_slot = jnp.where(slot == jnp.concatenate(ranks, axis=1), 1.0, 0.0).astype(BF16)
    owners = jnp.broadcast_to(owner[...].astype(F32), (SLOTS, 1024)).astype(BF16)

    def one_hot(o, now):
        onehot[pl.ds(pl.multiple_of(o * SLOTS, SLOTS), SLOTS), :] = jnp.where(
            owners == now, at_slot, jnp.zeros_like(at_slot)
        )
        return now + jnp.ones_like(now)

    lax.fori_loop(0, DEVICES, one_hot, jnp.zeros((SLOTS, 1024), BF16))

    source = lax.broadcasted_iota(jnp.int32, (2 * LANES, 2 * LANES), 0) & (LANES - 1)
    column = lax.broadcasted_iota(jnp.int32, (2 * LANES, 2 * LANES), 1)
    wanted = jnp.where(column < LANES, column + LANES - 1, column + 1) & (LANES - 1)
    by_one[...] = jnp.where(source == wanted, 1.0, 0.0).astype(BF16)


def advance(
    prob, row_low, row_high, plane_low, plane_high, corner_low, corner_high,
    t_r0, t_f1, t_r1, t_d, t_r2, t_f2, t_f3, t_n, t_mask, by_one, onehot, sent,
    u0, u1, u2, u3, xb, even, odd,
):
    zero = jnp.zeros((ALL, LANES), F32)
    for t in range(4):
        for u, ks in (
            (u0, (0, 12, 13, 14, 15, 16, 17)), (u1, (0, 13, 14, 15, 16, 17)), (u2, (0, 15, 16, 17)), (u3, (0, 15, 16, 17))
        ):
            for k in ks:
                u[t, k] = zero
    def prepare(n0, _):
        def put(t, row, count, values):
            rows = pl.ds(row, count)
            u0[t, n0 + 1, rows, :] = jnp.where(n0.astype(F32) < t_mask[t, rows, :], values, 0.0)

        for h in range(2):
            lanes = pl.ds(h * LANES, LANES)
            put(1 + h, FIRST, REACH, row_low[n0, pl.ds(FACE - REACH, REACH), lanes])
            put(1 + h, OWN + ROWS, REACH, row_high[n0, pl.ds(0, REACH), lanes])
            put(1 + h, OWN, ROWS, prob[n0, :, lanes])
        for t, plane, corner in ((0, plane_low, corner_low), (3, plane_high, corner_high)):
            put(t, FIRST, REACH, corner[n0, pl.ds(REACH, REACH), :])
            put(t, OWN + ROWS, REACH, corner[n0, pl.ds(0, REACH), :])
            put(t, OWN, ROWS, plane[n0])
        return 0

    lax.fori_loop(0, OLD0, prepare, 0)

    lane = lax.broadcasted_iota(jnp.int32, (8, LANES), 1)
    first_plane = lane < N4
    last_plane = lane >= LANES - N4

    def shift(q, src, n0, moved):
        tiles = (1, 2) if q == 3 else range(4)
        f3 = t_f3[q]
        for k in range(2):
            r3 = t_n[q, n0 + k, 0]
            rows = jnp.concatenate([src[a, n0 + k + 1, pl.ds(FIRST, WORK), :] for a in tiles], axis=0)
            high = rows.astype(BF16)
            low = (rows - high.astype(F32)).astype(BF16)
            both = jnp.dot(jnp.concatenate([high, low], axis=1), by_one[...], preferred_element_type=F32)
            both = both.reshape(-1, 8, 2 * LANES)
            flow = r3[None] * both[:, :, :LANES] + f3[None] * both[:, :, LANES:]
            moved[k, pl.ds(0, rows.shape[0]), :] = flow.reshape(rows.shape)

    def stage(q, src, dst):
        last = q == 3

        def update(n0, moved):
            pair = range(2)
            f0, l0, m0 = ([t_n[q, n0 + k, i] for k in pair] for i in (1, 2, 3))
            r2 = [t_r2[q, a] for a in range(4)]
            f2 = [t_f2[q, a] for a in range(4)]
            kept = {(k, a): [] for k in pair for a in (1, 2)}
            for g in range(8 if last else GROUPS):
                row = 8 * g + (OWN if last else FIRST)
                rows = pl.ds(row, 8)
                r0 = t_r0[q, rows, :]
                f1 = t_f1[q, rows, :]
                r0 = [r0 * m0[k] for k in pair]
                centre = [[src[a, n0 + k + 1, rows, :] for a in range(4)] for k in pair]
                up = [[pltpu.roll(c, N4, 1) for c in centre[k]] for k in pair]
                down = [[pltpu.roll(c, LANES - N4, 1) for c in centre[k]] for k in pair]
                for a in ((1, 2) if last else range(4)):
                    before = [src[a, n0, rows, :], centre[0][a]]
                    after = [centre[1][a], src[a, n0 + 3, rows, :]]
                    d = t_d[q, a, rows, :]
                    r1 = t_r1[q, a, rows, :]
                    place = pl.ds(WORK * (a - 1 if last else a) + row - FIRST, 8)
                    for k in pair:
                        c = centre[k][a]
                        from_below = jnp.where(first_plane, up[k][a - 1], up[k][a]) if a > 0 else up[k][a]
                        from_above = jnp.where(last_plane, down[k][a + 1], down[k][a]) if a < 3 else down[k][a]
                        acc = u0[a, n0 + k + 1, rows, :] + (d + l0[k]) * c
                        acc = acc + (r0[k] * before[k] + f0[k] * after[k])
                        acc = acc + (
                            r1 * src[a, n0 + k + 1, pl.ds(row - 1, 8), :]
                            + f1 * src[a, n0 + k + 1, pl.ds(row + 1, 8), :]
                        )
                        acc = acc + (r2[a] * from_below + f2[a] * from_above)
                        acc = acc + moved[k, place, :]
                        if last:
                            kept[k, a].append(acc)
                        else:
                            dst[a, n0 + k + 1, rows, :] = acc
                if last and g % 2 == 1:
                    for k in pair:
                        place = pl.ds(pl.multiple_of((n0 + k) * ROWS + 8 * (g - 1), 16), 16)
                        for a in (1, 2):
                            both = jnp.concatenate(kept[k, a], axis=0)
                            kept[k, a] = []
                            high = both.astype(BF16)
                            low = (both - high.astype(F32)).astype(BF16)
                            dst[place, pl.ds((a - 1) * LANES, LANES)] = high
                            dst[place, pl.ds((a + 1) * LANES, LANES)] = low

        def body(i, _):
            n0 = 4 * i
            shift(q, src, n0 + 2, odd)
            update(n0, even)
            shift(q, src, jnp.minimum(n0 + 4, N0 - 2), even)
            update(n0 + 2, odd)
            return 0

        shift(q, src, 0, even)
        lax.fori_loop(0, 4 if last else 3, body, 0)
        if q in (1, 2):
            update(12, even)

    stage(0, u0, u1)
    stage(1, u1, u2)
    stage(2, u2, u3)
    stage(3, u3, xb)

    def permute(i, _):
        place = pl.ds(pl.multiple_of(i * BLOCK, BLOCK), BLOCK)
        both = jnp.dot(onehot[place, :], xb[...], preferred_element_type=F32)
        sent[place, :] = both[:, :2 * LANES] + both[:, 2 * LANES:]
        return 0

    lax.fori_loop(0, DEVICES * SLOTS // BLOCK, permute, 0)


def ring(values, axis, shift):
    count = lax.axis_size(axis)
    return lax.ppermute(values, axis, [(i, (i + shift) % count) for i in range(count)])


def shards(probability, extent, slab_width, rate_const, hill_const, stoichiometry, new_owner):
    vmem = pltpu.VMEM
    field = probability[0]
    inner = field[:OLD0]
    plane_low = ring(inner[:, :, LANES:], "gy", 1)
    plane_high = ring(inner[:, :, :LANES], "gy", -1)
    params = jnp.concatenate(
        [extent.astype(F32), slab_width.astype(F32), rate_const, hill_const, stoichiometry.T.reshape(32).astype(F32)]
    )
    whole = pl.BlockSpec(memory_space=pltpu.VMEM)
    face = ((OLD0, FACE, PLANES * N4), F32)
    tables = [
        face,
        face,
        ((4, ALL, LANES), F32),
        ((4, ALL, LANES), F32),
        ((4, 4, ALL, LANES), F32),
        ((4, 4, ALL, LANES), F32),
        ((4, 4, 8, LANES), F32),
        ((4, 4, 8, LANES), F32),
        ((4, 8, LANES), F32),
        ((4, N0, 4, 8, LANES), F32),
        ((4, ALL, LANES), F32),
        ((2 * LANES, 2 * LANES), BF16),
        ((DEVICES * SLOTS, N0 * ROWS), BF16),
    ]
    go_up, go_down, *made = pl.pallas_call(
        prepare_tables,
        out_shape=[jax.ShapeDtypeStruct(*table) for table in tables],
        in_specs=[pl.BlockSpec(memory_space=pltpu.SMEM)] + [whole] * 3,
        out_specs=[whole] * len(tables),
        scratch_shapes=[vmem((128, 128), BF16), vmem((128, 128), BF16)],
        compiler_params=pltpu.CompilerParams(vmem_limit_bytes=12 * 1024 * 1024),
        cost_estimate=pl.CostEstimate(flops=10_000_000, bytes_accessed=16_000_000, transcendentals=0),
        name="prepare_tables",
    )(params, new_owner.reshape(1, N0 * ROWS), inner[:, ROWS - FACE:], inner[:, :FACE])
    row_low = ring(go_up, "gx", 1)
    row_high = ring(go_down, "gx", -1)
    corner = jnp.concatenate([row_high[:, :4], row_low[:, 4:]], axis=1)
    corner_low = ring(corner[:, :, LANES:], "gy", 1)
    corner_high = ring(corner[:, :, :LANES], "gy", -1)
    sent = pl.pallas_call(
        advance,
        out_shape=jax.ShapeDtypeStruct((DEVICES * SLOTS, PLANES * N4), F32),
        in_specs=[whole] * (7 + len(made)),
        out_specs=whole,
        scratch_shapes=[
            vmem((4, N0 + 2, ALL, LANES), F32),
            vmem((4, N0 + 2, ALL, LANES), F32),
            vmem((4, N0 + 2, ALL, LANES), F32),
            vmem((4, N0 + 2, ALL, LANES), F32),
            vmem((N0 * ROWS, 4 * LANES), BF16),
            vmem((2, 4 * WORK, LANES), F32),
            vmem((2, 4 * WORK, LANES), F32),
        ],
        compiler_params=pltpu.CompilerParams(vmem_limit_bytes=32 * 1024 * 1024),
        name="advance",
    )(field, row_low, row_high, plane_low, plane_high, corner_low, corner_high, *made)
    moved = lax.all_to_all(
        sent.reshape(DEVICES, SLOTS, PLANES * N4), ("gx", "gy"), split_axis=0, concat_axis=0, tiled=True
    )
    return moved[None]


def solution(mesh):
    in_specs = (P("gx", None, None, "gy"), P(), P(), P(), P(), P(), P("gx", "gy", None, None))
    out_specs = P(("gx", "gy"), None, None, None)
    return jax.shard_map(shards, mesh=mesh, in_specs=in_specs, out_specs=out_specs, check_vma=False)
```

```python
import functools

import jax
import jax.numpy as jnp
from jax import lax
from jax.experimental import pallas as pl
from jax.experimental.pallas import tpu as pltpu
from jax.sharding import PartitionSpec as P

MESH = pl.DeviceIdType.MESH
F32 = jnp.float32
BF16 = jnp.bfloat16

time_step = 0.15
GX, GY, DEVICES = 16, 8, 128
LATTICE = (16, 1024, 64, 32)
N0, ROWS, PLANES, N4 = 16, 64, 8, 32
LANES = 128
SLOTS = 16
OLD0 = 11
FACE = 8
REACH = 4
FIRST = 8
OWN = FIRST + REACH
GROUPS = 9
WORK = 8 * GROUPS
ALL = WORK + 2 * FIRST
BLOCK = 512


def prepare_tables(
    params, owner, last_rows, first_rows, go_up, go_down, t_r0, t_f1, t_r1, t_d, t_r2, t_f2, t_f3, t_n, t_mask, by_one, onehot, prefix, ones
):
    gx = lax.axis_index("gx")
    gy = lax.axis_index("gy")

    go_up[...] = last_rows[...]
    go_down[...] = first_rows[...]

    extent = [params[d] for d in range(4)]
    edge = [params[d] + params[4 + d] for d in range(4)]

    def pick(start, species, sign):
        total = jnp.float32(0.0)
        for r in range(8):
            total = total + jnp.where(params[24 + 8 * species + r] == sign, params[start + r], jnp.float32(0.0))
        return total

    rise_rate = [pick(8, d, 1.0) for d in range(4)]
    rise_hill = [pick(16, d, 1.0) for d in range(4)]
    fall_rate = [pick(8, d, -1.0) for d in range(4)]

    def rise(d, x):
        scaled = x / jnp.full(x.shape, rise_hill[d])
        return jnp.full(x.shape, rise_rate[d]) / (1.0 + scaled * scaled)

    def fall(d, x):
        return (2.0 * fall_rate[d]) * x

    def frac(n, d):
        return n.astype(F32) * (1.0 / LATTICE[d])

    steps = [time_step / j for j in (4.0, 3.0, 2.0, 1.0)]

    n1 = (gx * ROWS - OWN + LATTICE[1] + lax.broadcasted_iota(jnp.int32, (ALL, LANES), 0)) & (LATTICE[1] - 1)
    rise_0 = rise(0, frac(n1, 1))
    leave_1 = rise_0 + fall(1, frac(n1, 1))
    fall_1 = fall(1, frac((n1 + 1) & (LATTICE[1] - 1), 1))
    in_1 = jnp.where(n1.astype(F32) < edge[1], 1.0, 0.0)
    for q in range(4):
        t_r0[q] = steps[q] * rise_0
        t_f1[q] = steps[q] * fall_1
    lane8 = lax.broadcasted_iota(jnp.int32, (8, LANES), 1)
    n3 = lane8 & (N4 - 1)
    rise_2 = rise(2, frac(n3, 3))
    leave_3 = rise_2 + fall(3, frac(n3, 3))
    fall_3 = fall(3, frac((n3 + 1) & (N4 - 1), 3))
    in_3 = jnp.where(n3.astype(F32) < edge[3], 1.0, 0.0)
    for q in range(4):
        t_f3[q] = steps[q] * fall_3
    for t in range(4):
        n2 = (gy * PLANES + 4 * (t - 1) + LATTICE[2] + (lane8 >> 5)) & (LATTICE[2] - 1)
        rise_1 = rise(1, frac(n2, 2))
        leave_23 = leave_3 + rise_1 + fall(2, frac(n2, 2))
        fall_2 = fall(2, frac((n2 + 1) & (LATTICE[2] - 1), 2))
        in_2 = jnp.where(n2.astype(F32) < edge[2], 1.0, 0.0)
        old_23 = (n2.astype(F32) < extent[2]) & (n3.astype(F32) < extent[3])
        old_1 = n1.astype(F32) < extent[1]
        t_mask[t] = jnp.where(
            old_1 & jnp.concatenate([old_23] * (ALL // 8), axis=0), extent[0], 0.0
        )
        rise_1 = jnp.concatenate([rise_1] * (ALL // 8), axis=0)
        leave_23 = jnp.concatenate([leave_23] * (ALL // 8), axis=0)
        for q in range(4):
            t_r2[q, t] = steps[q] * (rise_2 * in_2)
            t_f2[q, t] = steps[q] * fall_2
            t_r1[q, t] = steps[q] * (rise_1 * in_1)
            t_d[q, t] = (-steps[q]) * (leave_1 + leave_23)

    def species_zero(n0, _):
        here = jnp.full((8, LANES), n0, jnp.int32)
        rise_3 = rise(3, frac(here, 0))
        leave_0 = rise_3 + fall(0, frac(here, 0))
        fall_0 = fall(0, frac(here + 1, 0))
        in_0 = jnp.where(here.astype(F32) < edge[0], 1.0, 0.0)
        for q in range(4):
            t_n[q, n0, 0] = steps[q] * (rise_3 * in_3)
            t_n[q, n0, 1] = steps[q] * fall_0
            t_n[q, n0, 2] = (-steps[q]) * leave_0
            t_n[q, n0, 3] = in_0
        return 0

    lax.fori_loop(0, N0, species_zero, 0)

    prefix[...] = jnp.where(
        lax.broadcasted_iota(jnp.int32, (128, 128), 0) < lax.broadcasted_iota(jnp.int32, (128, 128), 1), 1.0, 0.0
    ).astype(BF16)
    ones[...] = jnp.ones((128, 128), BF16)
    running = jnp.zeros((DEVICES, 128), F32)
    ranks = []
    peer = lax.broadcasted_iota(jnp.int32, (DEVICES, 128), 0)
    for b in range(8):
        part = owner[:, pl.ds(b * 128, 128)]
        hit = jnp.where(peer == part, 1.0, 0.0)
        hit16 = hit.astype(BF16)
        count = running + jnp.dot(hit16, prefix[...], preferred_element_type=F32)
        running = running + jnp.dot(hit16, ones[...], preferred_element_type=F32)
        rank = jnp.sum(hit * count, axis=0, keepdims=True)
        ranks.append(rank)

    slot = lax.broadcasted_iota(jnp.int32, (SLOTS, 1024), 0).astype(F32)
    at_slot = jnp.where(slot == jnp.concatenate(ranks, axis=1), 1.0, 0.0).astype(BF16)
    owners = jnp.broadcast_to(owner[...].astype(F32), (SLOTS, 1024)).astype(BF16)

    def one_hot(o, now):
        onehot[pl.ds(pl.multiple_of(o * SLOTS, SLOTS), SLOTS), :] = jnp.where(
            owners == now, at_slot, jnp.zeros_like(at_slot)
        )
        return now + jnp.ones_like(now)

    lax.fori_loop(0, DEVICES, one_hot, jnp.zeros((SLOTS, 1024), BF16))

    source = lax.broadcasted_iota(jnp.int32, (2 * LANES, 2 * LANES), 0) & (LANES - 1)
    column = lax.broadcasted_iota(jnp.int32, (2 * LANES, 2 * LANES), 1)
    wanted = jnp.where(column < LANES, column + LANES - 1, column + 1) & (LANES - 1)
    by_one[...] = jnp.where(source == wanted, 1.0, 0.0).astype(BF16)


def advance(
    prob, row_low, row_high, plane_low, plane_high, corner_low, corner_high,
    t_r0, t_f1, t_r1, t_d, t_r2, t_f2, t_f3, t_n, t_mask, by_one, onehot, sent,
    u0, u1, u2, u3, xb, even, odd,
):
    zero = jnp.zeros((ALL, LANES), F32)
    for t in range(4):
        for u, ks in (
            (u0, (0, 12, 13, 14, 15, 16, 17)), (u1, (0, 13, 14, 15, 16, 17)), (u2, (0, 15, 16, 17)), (u3, (0, 15, 16, 17))
        ):
            for k in ks:
                u[t, k] = zero
    row8 = lax.broadcasted_iota(jnp.int32, (8, LANES), 0)

    def prepare(n0, _):
        def put(t, row, count, values):
            rows = pl.ds(row, count)
            u0[t, n0 + 1, rows, :] = jnp.where(n0.astype(F32) < t_mask[t, rows, :], values, 0.0)

        for h in range(2):
            lanes = pl.ds(h * LANES, LANES)
            put(1 + h, FIRST, REACH, row_low[n0, pl.ds(FACE - REACH, REACH), lanes])
            put(1 + h, OWN + ROWS, REACH, row_high[n0, pl.ds(0, REACH), lanes])
            put(1 + h, OWN, ROWS, prob[n0, :, lanes])
        for t, plane, corner in ((0, plane_low, corner_low), (3, plane_high, corner_high)):
            wide = [jnp.broadcast_to(corner[n0, pl.ds(j, 1), :], (8, LANES)) for j in range(3)]
            turned = LANES - N4 if t == 0 else N4
            block = jnp.where(row8 == 3, wide[0], jnp.zeros((8, LANES), F32))
            block = jnp.where(row8 == 2, wide[1], block)
            block = jnp.where(row8 == 1, pltpu.roll(wide[0], turned, 1), block)
            block = jnp.where(row8 == 4, wide[2], block)
            block = jnp.where(row8 == 5, pltpu.roll(wide[1], 2 * N4, 1), block)
            block = jnp.where(row8 == 6, pltpu.roll(wide[2], turned, 1), block)
            put(t, FIRST, REACH, block[:REACH])
            put(t, OWN + ROWS, REACH, block[REACH:])
            put(t, OWN, ROWS, plane[n0])
        return 0

    lax.fori_loop(0, OLD0, prepare, 0, unroll=True)

    lane = lax.broadcasted_iota(jnp.int32, (8, LANES), 1)
    first_plane = lane < N4
    last_plane = lane >= LANES - N4

    def shift(q, src, n0, moved):
        tiles = (1, 2) if q == 3 else range(4)
        f3 = t_f3[q]
        for k in range(2):
            r3 = t_n[q, n0 + k, 0]
            rows = jnp.concatenate([src[a, n0 + k + 1, pl.ds(FIRST, WORK), :] for a in tiles], axis=0)
            high = rows.astype(BF16)
            low = (rows - high.astype(F32)).astype(BF16)
            both = jnp.dot(jnp.concatenate([high, low], axis=1), by_one[...], preferred_element_type=F32)
            both = both.reshape(-1, 8, 2 * LANES)
            flow = r3[None] * both[:, :, :LANES] + f3[None] * both[:, :, LANES:]
            moved[k, pl.ds(0, rows.shape[0]), :] = flow.reshape(rows.shape)

    def stage(q, src, dst):
        last = q == 3

        def update(n0, moved):
            pair = range(2)
            f0, l0, m0 = ([t_n[q, n0 + k, i] for k in pair] for i in (1, 2, 3))
            r2 = [t_r2[q, a] for a in range(4)]
            f2 = [t_f2[q, a] for a in range(4)]
            kept = {(k, a): [] for k in pair for a in (1, 2)}
            for g in range(8 if last else GROUPS):
                row = 8 * g + (OWN if last else FIRST)
                rows = pl.ds(row, 8)
                r0 = t_r0[q, rows, :]
                f1 = t_f1[q, rows, :]
                r0 = [r0 * m0[k] for k in pair]
                centre = [[src[a, n0 + k + 1, rows, :] for a in range(4)] for k in pair]
                up = [[pltpu.roll(c, N4, 1) for c in centre[k]] for k in pair]
                down = [[pltpu.roll(c, LANES - N4, 1) for c in centre[k]] for k in pair]
                for a in ((1, 2) if last else range(4)):
                    before = [src[a, n0, rows, :], centre[0][a]]
                    after = [centre[1][a], src[a, n0 + 3, rows, :]]
                    d = t_d[q, a, rows, :]
                    r1 = t_r1[q, a, rows, :]
                    place = pl.ds(WORK * (a - 1 if last else a) + row - FIRST, 8)
                    for k in pair:
                        c = centre[k][a]
                        from_below = jnp.where(first_plane, up[k][a - 1], up[k][a]) if a > 0 else up[k][a]
                        from_above = jnp.where(last_plane, down[k][a + 1], down[k][a]) if a < 3 else down[k][a]
                        acc = u0[a, n0 + k + 1, rows, :] + (d + l0[k]) * c
                        acc = acc + (r0[k] * before[k] + f0[k] * after[k])
                        acc = acc + (
                            r1 * src[a, n0 + k + 1, pl.ds(row - 1, 8), :]
                            + f1 * src[a, n0 + k + 1, pl.ds(row + 1, 8), :]
                        )
                        acc = acc + (r2[a] * from_below + f2[a] * from_above)
                        acc = acc + moved[k, place, :]
                        if last:
                            kept[k, a].append(acc)
                        else:
                            dst[a, n0 + k + 1, rows, :] = acc
                if last and g % 2 == 1:
                    for k in pair:
                        place = pl.ds(pl.multiple_of((n0 + k) * ROWS + 8 * (g - 1), 16), 16)
                        for a in (1, 2):
                            both = jnp.concatenate(kept[k, a], axis=0)
                            kept[k, a] = []
                            high = both.astype(BF16)
                            low = (both - high.astype(F32)).astype(BF16)
                            dst[place, pl.ds((a - 1) * LANES, LANES)] = high
                            dst[place, pl.ds((a + 1) * LANES, LANES)] = low

        def body(i, _):
            n0 = 4 * i
            shift(q, src, n0 + 2, odd)
            update(n0, even)
            shift(q, src, jnp.minimum(n0 + 4, N0 - 2), even)
            update(n0 + 2, odd)
            return 0

        shift(q, src, 0, even)
        lax.fori_loop(0, 4 if last else 3, body, 0)
        if q in (1, 2):
            update(12, even)

    stage(0, u0, u1)
    stage(1, u1, u2)
    stage(2, u2, u3)
    stage(3, u3, xb)

    def permute(i, _):
        place = pl.ds(pl.multiple_of(i * BLOCK, BLOCK), BLOCK)
        both = jnp.dot(onehot[place, :], xb[...], preferred_element_type=F32)
        sent[place, :] = both[:, :2 * LANES] + both[:, 2 * LANES:]
        return 0

    lax.fori_loop(0, DEVICES * SLOTS // BLOCK, permute, 0)


def pack_corners(row_low, row_high, to_above, to_below):
    lane = lax.broadcasted_iota(jnp.int32, (1, LANES), 1)
    for n0 in range(OLD0):
        for out, start, one in ((to_above, LANES, N4), (to_below, 0, LANES - N4)):
            low = row_low[n0, :, pl.ds(start, LANES)]
            high = row_high[n0, :, pl.ds(start, LANES)]
            up = start > 0
            far_one = lane < N4 if up else lane >= LANES - N4
            far_two = lane < 2 * N4 if up else lane >= 2 * N4
            out[n0, pl.ds(0, 1), :] = jnp.where(far_one, pltpu.roll(low, one, 1)[5:6], low[7:8])
            out[n0, pl.ds(1, 1), :] = jnp.where(far_two, pltpu.roll(high, 2 * N4, 1)[1:2], low[6:7])
            out[n0, pl.ds(2, 1), :] = jnp.where(far_one, pltpu.roll(high, one, 1)[2:3], high[0:1])


def ring(values, axis, shift):
    count = lax.axis_size(axis)
    return lax.ppermute(values, axis, [(i, (i + shift) % count) for i in range(count)])


def shards(probability, extent, slab_width, rate_const, hill_const, stoichiometry, new_owner):
    vmem = pltpu.VMEM
    field = probability[0]
    inner = field[:OLD0]
    plane_low = ring(inner[:, :, LANES:], "gy", 1)
    plane_high = ring(inner[:, :, :LANES], "gy", -1)
    params = jnp.concatenate(
        [extent.astype(F32), slab_width.astype(F32), rate_const, hill_const, stoichiometry.T.reshape(32).astype(F32)]
    )
    whole = pl.BlockSpec(memory_space=pltpu.VMEM)
    face = ((OLD0, FACE, PLANES * N4), F32)
    tables = [
        face,
        face,
        ((4, ALL, LANES), F32),
        ((4, ALL, LANES), F32),
        ((4, 4, ALL, LANES), F32),
        ((4, 4, ALL, LANES), F32),
        ((4, 4, 8, LANES), F32),
        ((4, 4, 8, LANES), F32),
        ((4, 8, LANES), F32),
        ((4, N0, 4, 8, LANES), F32),
        ((4, ALL, LANES), F32),
        ((2 * LANES, 2 * LANES), BF16),
        ((DEVICES * SLOTS, N0 * ROWS), BF16),
    ]
    go_up, go_down, *made = pl.pallas_call(
        prepare_tables,
        out_shape=[jax.ShapeDtypeStruct(*table) for table in tables],
        in_specs=[pl.BlockSpec(memory_space=pltpu.SMEM)] + [whole] * 3,
        out_specs=[whole] * len(tables),
        scratch_shapes=[vmem((128, 128), BF16), vmem((128, 128), BF16)],
        compiler_params=pltpu.CompilerParams(vmem_limit_bytes=12 * 1024 * 1024),
        cost_estimate=pl.CostEstimate(flops=10_000_000, bytes_accessed=16_000_000, transcendentals=0),
        name="prepare_tables",
    )(params, new_owner.reshape(1, N0 * ROWS), inner[:, ROWS - FACE:], inner[:, :FACE])
    row_low = ring(go_up, "gx", 1)
    row_high = ring(go_down, "gx", -1)
    corner = jax.ShapeDtypeStruct((OLD0, 3, LANES), F32)
    to_above, to_below = pl.pallas_call(
        pack_corners,
        out_shape=[corner, corner],
        in_specs=[whole, whole],
        out_specs=[whole, whole],
        compiler_params=pltpu.CompilerParams(vmem_limit_bytes=4 * 1024 * 1024),
        name="pack_corners",
    )(row_low, row_high)
    corner_low = ring(to_above, "gy", 1)
    corner_high = ring(to_below, "gy", -1)
    sent = pl.pallas_call(
        advance,
        out_shape=jax.ShapeDtypeStruct((DEVICES * SLOTS, PLANES * N4), F32),
        in_specs=[whole] * (7 + len(made)),
        out_specs=whole,
        scratch_shapes=[
            vmem((4, N0 + 2, ALL, LANES), F32),
            vmem((4, N0 + 2, ALL, LANES), F32),
            vmem((4, N0 + 2, ALL, LANES), F32),
            vmem((4, N0 + 2, ALL, LANES), F32),
            vmem((N0 * ROWS, 4 * LANES), BF16),
            vmem((2, 4 * WORK, LANES), F32),
            vmem((2, 4 * WORK, LANES), F32),
        ],
        compiler_params=pltpu.CompilerParams(vmem_limit_bytes=32 * 1024 * 1024),
        name="advance",
    )(field, row_low, row_high, plane_low, plane_high, corner_low, corner_high, *made)
    moved = lax.all_to_all(
        sent.reshape(DEVICES, SLOTS, PLANES * N4), ("gx", "gy"), split_axis=0, concat_axis=0, tiled=True
    )
    return moved[None]


def solution(mesh):
    in_specs = (P("gx", None, None, "gy"), P(), P(), P(), P(), P(), P("gx", "gy", None, None))
    out_specs = P(("gx", "gy"), None, None, None)
    return jax.shard_map(shards, mesh=mesh, in_specs=in_specs, out_specs=out_specs, check_vma=False)
```

```python
import functools

import jax
import jax.numpy as jnp
from jax import lax
from jax.experimental import pallas as pl
from jax.experimental.pallas import tpu as pltpu
from jax.sharding import PartitionSpec as P

MESH = pl.DeviceIdType.MESH
F32 = jnp.float32
BF16 = jnp.bfloat16

time_step = 0.15
GX, GY, DEVICES = 16, 8, 128
LATTICE = (16, 1024, 64, 32)
N0, ROWS, PLANES, N4 = 16, 64, 8, 32
LANES = 128
SLOTS = 16
OLD0 = 11
FACE = 8
REACH = 4
FIRST = 8
OWN = FIRST + REACH
GROUPS = 9
WORK = 8 * GROUPS
ALL = WORK + 2 * FIRST
BLOCK = 1024


def prepare_tables(
    params, owner, last_rows, first_rows, go_up, go_down, t_r0, t_f1, t_r1, t_d, t_r2, t_f2, t_f3, t_n, t_mask, by_one, onehot, prefix, ones
):
    gx = lax.axis_index("gx")
    gy = lax.axis_index("gy")

    go_up[...] = last_rows[...]
    go_down[...] = first_rows[...]

    extent = [params[d] for d in range(4)]
    edge = [params[d] + params[4 + d] for d in range(4)]

    def pick(start, species, sign):
        total = jnp.float32(0.0)
        for r in range(8):
            total = total + jnp.where(params[24 + 8 * species + r] == sign, params[start + r], jnp.float32(0.0))
        return total

    rise_rate = [pick(8, d, 1.0) for d in range(4)]
    rise_hill = [pick(16, d, 1.0) for d in range(4)]
    fall_rate = [pick(8, d, -1.0) for d in range(4)]

    def rise(d, x):
        scaled = x / jnp.full(x.shape, rise_hill[d])
        return jnp.full(x.shape, rise_rate[d]) / (1.0 + scaled * scaled)

    def fall(d, x):
        return (2.0 * fall_rate[d]) * x

    def frac(n, d):
        return n.astype(F32) * (1.0 / LATTICE[d])

    steps = [time_step / j for j in (4.0, 3.0, 2.0, 1.0)]

    n1 = (gx * ROWS - OWN + LATTICE[1] + lax.broadcasted_iota(jnp.int32, (ALL, LANES), 0)) & (LATTICE[1] - 1)
    rise_0 = rise(0, frac(n1, 1))
    leave_1 = rise_0 + fall(1, frac(n1, 1))
    fall_1 = fall(1, frac((n1 + 1) & (LATTICE[1] - 1), 1))
    in_1 = jnp.where(n1.astype(F32) < edge[1], 1.0, 0.0)
    for q in range(4):
        t_r0[q] = steps[q] * rise_0
        t_f1[q] = steps[q] * fall_1
    lane8 = lax.broadcasted_iota(jnp.int32, (8, LANES), 1)
    n3 = lane8 & (N4 - 1)
    rise_2 = rise(2, frac(n3, 3))
    leave_3 = rise_2 + fall(3, frac(n3, 3))
    fall_3 = fall(3, frac((n3 + 1) & (N4 - 1), 3))
    in_3 = jnp.where(n3.astype(F32) < edge[3], 1.0, 0.0)
    for q in range(4):
        t_f3[q] = steps[q] * fall_3
    for t in range(4):
        n2 = (gy * PLANES + 4 * (t - 1) + LATTICE[2] + (lane8 >> 5)) & (LATTICE[2] - 1)
        rise_1 = rise(1, frac(n2, 2))
        leave_23 = leave_3 + rise_1 + fall(2, frac(n2, 2))
        fall_2 = fall(2, frac((n2 + 1) & (LATTICE[2] - 1), 2))
        in_2 = jnp.where(n2.astype(F32) < edge[2], 1.0, 0.0)
        old_23 = (n2.astype(F32) < extent[2]) & (n3.astype(F32) < extent[3])
        old_1 = n1.astype(F32) < extent[1]
        t_mask[t] = jnp.where(
            old_1 & jnp.concatenate([old_23] * (ALL // 8), axis=0), extent[0], 0.0
        )
        rise_1 = jnp.concatenate([rise_1] * (ALL // 8), axis=0)
        leave_23 = jnp.concatenate([leave_23] * (ALL // 8), axis=0)
        for q in range(4):
            t_r2[q, t] = steps[q] * (rise_2 * in_2)
            t_f2[q, t] = steps[q] * fall_2
            t_r1[q, t] = steps[q] * (rise_1 * in_1)
            t_d[q, t] = (-steps[q]) * (leave_1 + leave_23)

    def species_zero(n0, _):
        here = jnp.full((8, LANES), n0, jnp.int32)
        rise_3 = rise(3, frac(here, 0))
        leave_0 = rise_3 + fall(0, frac(here, 0))
        fall_0 = fall(0, frac(here + 1, 0))
        in_0 = jnp.where(here.astype(F32) < edge[0], 1.0, 0.0)
        for q in range(4):
            t_n[q, n0, 0] = steps[q] * (rise_3 * in_3)
            t_n[q, n0, 1] = steps[q] * fall_0
            t_n[q, n0, 2] = (1.0 if q == 0 else 0.0) - steps[q] * leave_0
            t_n[q, n0, 3] = in_0
        return 0

    lax.fori_loop(0, N0, species_zero, 0)

    prefix[...] = jnp.where(
        lax.broadcasted_iota(jnp.int32, (128, 128), 0) < lax.broadcasted_iota(jnp.int32, (128, 128), 1), 1.0, 0.0
    ).astype(BF16)
    ones[...] = jnp.ones((128, 128), BF16)
    running = jnp.zeros((DEVICES, 128), F32)
    ranks = []
    peer = lax.broadcasted_iota(jnp.int32, (DEVICES, 128), 0)
    for b in range(8):
        part = owner[:, pl.ds(b * 128, 128)]
        hit = jnp.where(peer == part, 1.0, 0.0)
        hit16 = hit.astype(BF16)
        count = running + jnp.dot(hit16, prefix[...], preferred_element_type=F32)
        running = running + jnp.dot(hit16, ones[...], preferred_element_type=F32)
        rank = jnp.sum(hit * count, axis=0, keepdims=True)
        ranks.append(rank)

    slot = lax.broadcasted_iota(jnp.int32, (SLOTS, 1024), 0).astype(F32)
    at_slot = jnp.where(slot == jnp.concatenate(ranks, axis=1), 1.0, 0.0).astype(BF16)
    owners = jnp.broadcast_to(owner[...].astype(F32), (SLOTS, 1024)).astype(BF16)

    def one_hot(o, now):
        onehot[pl.ds(pl.multiple_of(o * SLOTS, SLOTS), SLOTS), :] = jnp.where(
            owners == now, at_slot, jnp.zeros_like(at_slot)
        )
        return now + jnp.ones_like(now)

    lax.fori_loop(0, DEVICES, one_hot, jnp.zeros((SLOTS, 1024), BF16))

    source = lax.broadcasted_iota(jnp.int32, (2 * LANES, 2 * LANES), 0) & (LANES - 1)
    column = lax.broadcasted_iota(jnp.int32, (2 * LANES, 2 * LANES), 1)
    wanted = jnp.where(column < LANES, column + LANES - 1, column + 1) & (LANES - 1)
    by_one[...] = jnp.where(source == wanted, 1.0, 0.0).astype(BF16)


def advance(
    prob, row_low, row_high, plane_low, plane_high, corner_low, corner_high,
    t_r0, t_f1, t_r1, t_d, t_r2, t_f2, t_f3, t_n, t_mask, by_one, onehot, sent,
    u0, u1, u2, u3, xb, even, odd,
):
    zero = jnp.zeros((ALL, LANES), F32)
    for t in range(4):
        for u, ks in (
            (u0, (0, 12, 13, 14, 15, 16, 17)), (u1, (0, 13, 14, 15, 16, 17)), (u2, (0, 15, 16, 17)), (u3, (0, 15, 16, 17))
        ):
            for k in ks:
                u[t, k] = zero
    row8 = lax.broadcasted_iota(jnp.int32, (8, LANES), 0)

    def prepare(n0, _):
        def put(t, row, count, values):
            rows = pl.ds(row, count)
            u0[t, n0 + 1, rows, :] = jnp.where(n0.astype(F32) < t_mask[t, rows, :], values, 0.0)

        for h in range(2):
            lanes = pl.ds(h * LANES, LANES)
            put(1 + h, FIRST, REACH, row_low[n0, pl.ds(FACE - REACH, REACH), lanes])
            put(1 + h, OWN + ROWS, REACH, row_high[n0, pl.ds(0, REACH), lanes])
            put(1 + h, OWN, ROWS, prob[n0, :, lanes])
        for t, plane, corner in ((0, plane_low, corner_low), (3, plane_high, corner_high)):
            wide = [jnp.broadcast_to(corner[n0, pl.ds(j, 1), :], (8, LANES)) for j in range(3)]
            turned = LANES - N4 if t == 0 else N4
            block = jnp.where(row8 == 3, wide[0], jnp.zeros((8, LANES), F32))
            block = jnp.where(row8 == 2, wide[1], block)
            block = jnp.where(row8 == 1, pltpu.roll(wide[0], turned, 1), block)
            block = jnp.where(row8 == 4, wide[2], block)
            block = jnp.where(row8 == 5, pltpu.roll(wide[1], 2 * N4, 1), block)
            block = jnp.where(row8 == 6, pltpu.roll(wide[2], turned, 1), block)
            put(t, FIRST, REACH, block[:REACH])
            put(t, OWN + ROWS, REACH, block[REACH:])
            put(t, OWN, ROWS, plane[n0])
        return 0

    lax.fori_loop(0, OLD0, prepare, 0, unroll=True)

    lane = lax.broadcasted_iota(jnp.int32, (8, LANES), 1)
    first_plane = lane < N4
    last_plane = lane >= LANES - N4

    def shift(q, src, n0, moved):
        tiles = (1, 2) if q == 3 else range(4)
        f3 = t_f3[q]
        for k in range(2):
            r3 = t_n[q, n0 + k, 0]
            rows = jnp.concatenate([src[a, n0 + k + 1, pl.ds(FIRST, WORK), :] for a in tiles], axis=0)
            high = rows.astype(BF16)
            low = (rows - high.astype(F32)).astype(BF16)
            both = jnp.dot(jnp.concatenate([high, low], axis=1), by_one[...], preferred_element_type=F32)
            both = both.reshape(-1, 8, 2 * LANES)
            flow = r3[None] * both[:, :, :LANES] + f3[None] * both[:, :, LANES:]
            moved[k, pl.ds(0, rows.shape[0]), :] = flow.reshape(rows.shape)

    def stage(q, src, dst):
        last = q == 3

        def update(n0, moved):
            pair = range(2)
            f0, l0, m0 = ([t_n[q, n0 + k, i] for k in pair] for i in (1, 2, 3))
            r2 = [t_r2[q, a] for a in range(4)]
            f2 = [t_f2[q, a] for a in range(4)]
            kept = {(k, a): [] for k in pair for a in (1, 2)}
            for g in range(8 if last else GROUPS):
                row = 8 * g + (OWN if last else FIRST)
                rows = pl.ds(row, 8)
                r0 = t_r0[q, rows, :]
                f1 = t_f1[q, rows, :]
                r0 = [r0 * m0[k] for k in pair]
                centre = [[src[a, n0 + k + 1, rows, :] for a in range(4)] for k in pair]
                up = [[pltpu.roll(c, N4, 1) for c in centre[k]] for k in pair]
                down = [[pltpu.roll(c, LANES - N4, 1) for c in centre[k]] for k in pair]
                for a in ((1, 2) if last else range(4)):
                    before = [src[a, n0, rows, :], centre[0][a]]
                    after = [centre[1][a], src[a, n0 + 3, rows, :]]
                    d = t_d[q, a, rows, :]
                    r1 = t_r1[q, a, rows, :]
                    place = pl.ds(WORK * (a - 1 if last else a) + row - FIRST, 8)
                    for k in pair:
                        c = centre[k][a]
                        from_below = jnp.where(first_plane, up[k][a - 1], up[k][a]) if a > 0 else up[k][a]
                        from_above = jnp.where(last_plane, down[k][a + 1], down[k][a]) if a < 3 else down[k][a]
                        acc = (d + l0[k]) * c
                        if q > 0:
                            acc = u0[a, n0 + k + 1, rows, :] + acc
                        acc = acc + (r0[k] * before[k] + f0[k] * after[k])
                        acc = acc + (
                            r1 * src[a, n0 + k + 1, pl.ds(row - 1, 8), :]
                            + f1 * src[a, n0 + k + 1, pl.ds(row + 1, 8), :]
                        )
                        acc = acc + (r2[a] * from_below + f2[a] * from_above)
                        acc = acc + moved[k, place, :]
                        if last:
                            kept[k, a].append(acc)
                        else:
                            dst[a, n0 + k + 1, rows, :] = acc
                if last and g % 2 == 1:
                    for k in pair:
                        place = pl.ds(pl.multiple_of((n0 + k) * ROWS + 8 * (g - 1), 16), 16)
                        for a in (1, 2):
                            both = jnp.concatenate(kept[k, a], axis=0)
                            kept[k, a] = []
                            high = both.astype(BF16)
                            low = (both - high.astype(F32)).astype(BF16)
                            dst[place, pl.ds((a - 1) * LANES, LANES)] = high
                            dst[place, pl.ds((a + 1) * LANES, LANES)] = low

        def body(i, _):
            n0 = 4 * i
            shift(q, src, n0 + 2, odd)
            update(n0, even)
            shift(q, src, jnp.minimum(n0 + 4, N0 - 2), even)
            update(n0 + 2, odd)
            return 0

        shift(q, src, 0, even)
        lax.fori_loop(0, 4 if last else 3, body, 0)
        if q in (1, 2):
            update(12, even)

    stage(0, u0, u1)
    stage(1, u1, u2)
    stage(2, u2, u3)
    stage(3, u3, xb)

    def permute(i, _):
        place = pl.ds(pl.multiple_of(i * BLOCK, BLOCK), BLOCK)
        both = jnp.dot(onehot[place, :], xb[...], preferred_element_type=F32)
        sent[place, :] = both[:, :2 * LANES] + both[:, 2 * LANES:]
        return 0

    lax.fori_loop(0, DEVICES * SLOTS // BLOCK, permute, 0)


def pack_corners(row_low, row_high, to_above, to_below):
    lane = lax.broadcasted_iota(jnp.int32, (1, LANES), 1)
    for n0 in range(OLD0):
        for out, start, one in ((to_above, LANES, N4), (to_below, 0, LANES - N4)):
            low = row_low[n0, :, pl.ds(start, LANES)]
            high = row_high[n0, :, pl.ds(start, LANES)]
            up = start > 0
            far_one = lane < N4 if up else lane >= LANES - N4
            far_two = lane < 2 * N4 if up else lane >= 2 * N4
            out[n0, pl.ds(0, 1), :] = jnp.where(far_one, pltpu.roll(low, one, 1)[5:6], low[7:8])
            out[n0, pl.ds(1, 1), :] = jnp.where(far_two, pltpu.roll(high, 2 * N4, 1)[1:2], low[6:7])
            out[n0, pl.ds(2, 1), :] = jnp.where(far_one, pltpu.roll(high, one, 1)[2:3], high[0:1])


def ring(values, axis, shift):
    count = lax.axis_size(axis)
    return lax.ppermute(values, axis, [(i, (i + shift) % count) for i in range(count)])


def shards(probability, extent, slab_width, rate_const, hill_const, stoichiometry, new_owner):
    vmem = pltpu.VMEM
    field = probability[0]
    inner = field[:OLD0]
    plane_low = ring(inner[:, :, LANES:], "gy", 1)
    plane_high = ring(inner[:, :, :LANES], "gy", -1)
    params = jnp.concatenate(
        [extent.astype(F32), slab_width.astype(F32), rate_const, hill_const, stoichiometry.T.reshape(32).astype(F32)]
    )
    whole = pl.BlockSpec(memory_space=pltpu.VMEM)
    face = ((OLD0, FACE, PLANES * N4), F32)
    tables = [
        face,
        face,
        ((4, ALL, LANES), F32),
        ((4, ALL, LANES), F32),
        ((4, 4, ALL, LANES), F32),
        ((4, 4, ALL, LANES), F32),
        ((4, 4, 8, LANES), F32),
        ((4, 4, 8, LANES), F32),
        ((4, 8, LANES), F32),
        ((4, N0, 4, 8, LANES), F32),
        ((4, ALL, LANES), F32),
        ((2 * LANES, 2 * LANES), BF16),
        ((DEVICES * SLOTS, N0 * ROWS), BF16),
    ]
    go_up, go_down, *made = pl.pallas_call(
        prepare_tables,
        out_shape=[jax.ShapeDtypeStruct(*table) for table in tables],
        in_specs=[pl.BlockSpec(memory_space=pltpu.SMEM)] + [whole] * 3,
        out_specs=[whole] * len(tables),
        scratch_shapes=[vmem((128, 128), BF16), vmem((128, 128), BF16)],
        compiler_params=pltpu.CompilerParams(vmem_limit_bytes=12 * 1024 * 1024),
        cost_estimate=pl.CostEstimate(flops=10_000_000, bytes_accessed=16_000_000, transcendentals=0),
        name="prepare_tables",
    )(params, new_owner.reshape(1, N0 * ROWS), inner[:, ROWS - FACE:], inner[:, :FACE])
    row_low = ring(go_up, "gx", 1)
    row_high = ring(go_down, "gx", -1)
    corner = jax.ShapeDtypeStruct((OLD0, 3, LANES), F32)
    to_above, to_below = pl.pallas_call(
        pack_corners,
        out_shape=[corner, corner],
        in_specs=[whole, whole],
        out_specs=[whole, whole],
        compiler_params=pltpu.CompilerParams(vmem_limit_bytes=4 * 1024 * 1024),
        name="pack_corners",
    )(row_low, row_high)
    corner_low = ring(to_above, "gy", 1)
    corner_high = ring(to_below, "gy", -1)
    sent = pl.pallas_call(
        advance,
        out_shape=jax.ShapeDtypeStruct((DEVICES * SLOTS, PLANES * N4), F32),
        in_specs=[whole] * (7 + len(made)),
        out_specs=whole,
        scratch_shapes=[
            vmem((4, N0 + 2, ALL, LANES), F32),
            vmem((4, N0 + 2, ALL, LANES), F32),
            vmem((4, N0 + 2, ALL, LANES), F32),
            vmem((4, N0 + 2, ALL, LANES), F32),
            vmem((N0 * ROWS, 4 * LANES), BF16),
            vmem((2, 4 * WORK, LANES), F32),
            vmem((2, 4 * WORK, LANES), F32),
        ],
        compiler_params=pltpu.CompilerParams(vmem_limit_bytes=32 * 1024 * 1024),
        name="advance",
    )(field, row_low, row_high, plane_low, plane_high, corner_low, corner_high, *made)
    moved = lax.all_to_all(
        sent.reshape(DEVICES, SLOTS, PLANES * N4), ("gx", "gy"), split_axis=0, concat_axis=0, tiled=True
    )
    return moved[None]


def solution(mesh):
    in_specs = (P("gx", None, None, "gy"), P(), P(), P(), P(), P(), P("gx", "gy", None, None))
    out_specs = P(("gx", "gy"), None, None, None)
    return jax.shard_map(shards, mesh=mesh, in_specs=in_specs, out_specs=out_specs, check_vma=False)
```
